32 devices in a mesh: group: 2 (over y), ctx: 4 (over z), smp: 2 (over x), head: 2 (over core).
Axes of the slice: x: 2, y: 2, z: 4, core: 2. Of those that a mesh axis runs over, the one named last changes fastest.
Arguments:
- queries: bfloat16 [512, 2, 4096], P(('group', 'smp'), 'head'), parts along dimension 0, may hold values from -8 to 8
- prefix_cache: bfloat16 [2, 8192, 2, 512], P(None, ('group', 'ctx'), 'head'), parts along dimension 1, may hold values from -8 to 8
- suffix_cache: bfloat16 [2, 512, 128, 2, 512], P(None, ('group', 'ctx', 'smp'), None, 'head'), parts along dimension 1, may hold values from -8 to 8
- suffix_length: int32 [512], P(('group', 'smp')), parts along dimension 0, may hold values from 1 to 128, as said below
- cache_sample: int32 [512], P('group'), parts along dimension 0, may hold values from 0 to 255, as said below
- residual: bfloat16 [512, 8192], P(('group', 'ctx', 'head'), 'smp'), parts along dimension 0, may hold values from -6 to 6
- w_out: bfloat16 [2, 4096, 8192], P('head', 'ctx', 'smp'), may hold values from -0.75 to 0.75
- norm_gain: float32 [8192], P('smp'), may hold values from 0.1 to 1.9
- gate_matrix: bfloat16 [8192, 16384], P('smp', ('ctx', 'head')), may hold values from -0.0625 to 0.0625
- w_up: bfloat16 [8192, 16384], P('smp', ('ctx', 'head')), may hold values from -0.0625 to 0.0625
- w_down: bfloat16 [16384, 8192], P(('ctx', 'head'), 'smp'), may hold values from -0.046875 to 0.046875
Outputs:
- mixed: bfloat16 [512, 8192], P(('group', 'ctx', 'head'), 'smp'), parts along dimension 0
The draws below stay inside these ranges and needn't reach their ends.
There are 2 independent parts, one for each index of `group`. The reference program is written for one: setup_inputs(seed, part) draws one part's arguments, and reference() takes and returns one part's arrays. A program takes and returns all parts, laid end to end along the dimension named above; an argument that names none is the same for every part. Nothing has to cross between parts.
Inputs may be any that keep to these rules, and one draw needn't show every extreme that they name: `suffix_length`: the longest is exactly 128 in every draw. A permutation; cache row r and sample cache_sample[r] lie in the same group, the group of row r being (r // 32) % (2) and that of sample i being i // 128.
All inputs are finite; a program needn't handle non-finite values.
Results may differ from the reference program's by a relative error of at most 0.012.
Values may be sent and summed in bfloat16 or wider, within the bound.
No kernel may reach another device: no remote copies, remote signals or barrier semaphores. Data moves between devices by JAX's collectives and lax.ppermute only.
A program may use at most 192 MiB of HBM per device.

```python
import jax
import jax.numpy as jnp
from jax import lax

D = 8192
QUERY_HEADS = 64
KEY_VALUE_HEADS = 8
HD = 128
FF = 16384
SAMP_GRP = 128
PRE_DEV = 1024
SUFFIX = 128
HEAD_GROUP_COUNT = 2
QW = 4096
KVW = 512
PREFIX = 4096
SAMPLES = 256
ROWS_DEV = 32
N_CTX = 4


def drawn_draw(key):
    query_key = jax.random.fold_in(key, 11)
    cache_key = jax.random.fold_in(key, 12)
    value_key = jax.random.fold_in(key, 13)
    query_shape = (SAMPLES, HEAD_GROUP_COUNT, QW)
    cache_shape = (PREFIX, HEAD_GROUP_COUNT, KVW)
    queries = jnp.clip(jax.random.normal(query_key, query_shape, jnp.float32), -6.0, 6.0)
    prefix_keys = jnp.clip(1.5 * jax.random.normal(cache_key, cache_shape, jnp.float32), -8.0, 8.0)
    prefix_values = jnp.clip(jax.random.normal(value_key, cache_shape, jnp.float32), -6.0, 6.0)
    return (queries, jnp.stack([prefix_keys, prefix_values]))


def draw_queries(key, part):
    return drawn_draw(key)[0].astype(jnp.bfloat16)


def draw_prefix_cache(key, part):
    return drawn_draw(key)[1].astype(jnp.bfloat16)


def draw_suffix_length(key, part):
    lengths = jax.random.randint(jax.random.fold_in(key, 21), (SAMPLES,), 1, SUFFIX + 1)
    longest = jax.random.randint(jax.random.fold_in(key, 22), (), 0, SAMPLES)
    return lengths.at[longest].set(SUFFIX).astype(jnp.int32)


def draw_cache_sample(key, part):
    groups = SAMPLES // SAMP_GRP
    row_ids = jnp.arange(SAMPLES, dtype=jnp.int32)
    group_of_row = row_ids // ROWS_DEV % groups
    rank = row_ids // (ROWS_DEV * groups) * ROWS_DEV + row_ids % ROWS_DEV
    orders = jnp.stack([jax.random.permutation(jax.random.fold_in(key, 31 + number), SAMP_GRP) for number in range(groups)])
    return (group_of_row * SAMP_GRP + orders[group_of_row, rank]).astype(jnp.int32)


def draw_suffix_cache(key, part):
    cache_shape = (2, SAMPLES, SUFFIX, HEAD_GROUP_COUNT, KVW)
    cache_key = jax.random.fold_in(key, 41)
    cache = jnp.clip(3.0 * jax.random.normal(cache_key, cache_shape, jnp.float32), -5.0, 5.0)
    return cache.astype(jnp.bfloat16)


def levels(stream_key, dims, cuts, smallest, top_value):
    factor_of = 1.0
    for axis_at, blocks in cuts:
        draws = jax.random.uniform(jax.random.fold_in(jax.random.fold_in(stream_key, 6), axis_at), (blocks,), jnp.float32, smallest / len(cuts), top_value / len(cuts))
        factor_of = factor_of * jnp.repeat(jnp.exp(draws), dims[axis_at] // blocks).reshape((-1,) + (1,) * (len(dims) - 1 - axis_at))
    return factor_of


def normal_values(own_key, extent, spread, limit, pieces=(), kind=jnp.bfloat16):
    entries = spread * jax.random.normal(own_key, extent, jnp.float32)
    if pieces:
        entries = entries * levels(own_key, extent, pieces, -0.22, 0.18)
    return jnp.clip(entries, -limit, limit).astype(kind)


def setup_inputs(seed: int = 0, part: int = 0) -> dict:
    arg_keys = jax.random.split(jax.random.key(seed), 12)
    part_splits = jax.random.split(jax.random.fold_in(arg_keys[11], part), 12)
    return {
        "queries": draw_queries(jax.random.fold_in(jax.random.fold_in(arg_keys[11], part), 71), part),
        "prefix_cache": draw_prefix_cache(jax.random.fold_in(jax.random.fold_in(arg_keys[11], part), 71), part),
        "suffix_cache": draw_suffix_cache(jax.random.fold_in(jax.random.fold_in(arg_keys[11], part), 71), part),
        "suffix_length": draw_suffix_length(jax.random.fold_in(jax.random.fold_in(arg_keys[11], part), 71), part),
        "cache_sample": draw_cache_sample(jax.random.fold_in(jax.random.fold_in(arg_keys[11], part), 71), part),
        "residual": normal_values(part_splits[5], (SAMPLES, D), 1.0, 6.0, ((0, 8), (1, 2))),
        "w_out": normal_values(arg_keys[6], (HEAD_GROUP_COUNT, QW, D), (QUERY_HEADS * HD // 128) ** -0.5, 0.75, ((0, 2), (1, 4), (2, 2))),
        "norm_gain": jnp.clip(1.0 + 0.18 * jax.random.normal(arg_keys[7], (D,), jnp.float32), 0.1, 1.9),
        "gate_matrix": normal_values(arg_keys[8], (D, FF), D ** -0.5, 0.0625, ((0, 2), (1, 8))),
        "w_up": normal_values(arg_keys[9], (D, FF), D ** -0.5, 0.0625, ((0, 2), (1, 8))),
        "w_down": normal_values(arg_keys[10], (FF, D), FF ** -0.5, 0.046875, ((0, 8), (1, 2))),
    }


EPSILON = 1e-05

def finish_piece(scores, values, form):
    highest = lax.optimization_barrier(jnp.max(scores, axis=-1))
    weights = jnp.exp(scores - highest[..., None])
    totals = lax.optimization_barrier(jnp.sum(weights, axis=-1))
    rounded = lax.optimization_barrier(weights.astype(jnp.bfloat16)).astype(jnp.float32)
    summed = jnp.einsum(form, rounded, values)
    piece_out = (summed / totals[..., None]).astype(jnp.bfloat16)
    return (piece_out, highest + jnp.log(totals))

def reference(queries, prefix_cache, suffix_cache, suffix_length, cache_sample, residual, w_out, norm_gain, gate_matrix, w_up, w_down):
    key_value_heads_here = KEY_VALUE_HEADS // HEAD_GROUP_COUNT
    queries_per_key_value = QUERY_HEADS // KEY_VALUE_HEADS
    score_scale = HD ** (-0.5)
    query_rows = queries.astype(jnp.float32).reshape(SAMPLES, HEAD_GROUP_COUNT, key_value_heads_here, queries_per_key_value, HD)
    prefix_keys = prefix_cache[0].astype(jnp.float32).reshape(PREFIX, HEAD_GROUP_COUNT, key_value_heads_here, HD)
    prefix_values = prefix_cache[1].astype(jnp.float32).reshape(PREFIX, HEAD_GROUP_COUNT, key_value_heads_here, HD)

    def block_piece(block):
        start_pos = (block * PRE_DEV).astype(jnp.int32)
        block_keys = lax.dynamic_slice_in_dim(prefix_keys, start_pos, PRE_DEV, 0)
        block_values = lax.dynamic_slice_in_dim(prefix_values, start_pos, PRE_DEV, 0)
        scores = jnp.einsum('shjgd,phjd->shjgp', query_rows, block_keys) * score_scale
        return finish_piece(scores, block_values, 'shjgp,phjd->shjgd')
    block_out, block_lse = lax.map(block_piece, jnp.arange(N_CTX, dtype=jnp.int32))
    row_of = jnp.zeros((SAMPLES,), jnp.int32).at[cache_sample].set(jnp.arange(SAMPLES, dtype=jnp.int32))
    own_cache = jnp.take(suffix_cache, row_of, axis=1)
    suffix_keys = own_cache[0].astype(jnp.float32).reshape(SAMPLES, SUFFIX, HEAD_GROUP_COUNT, key_value_heads_here, HD)
    suffix_values = own_cache[1].astype(jnp.float32).reshape(SAMPLES, SUFFIX, HEAD_GROUP_COUNT, key_value_heads_here, HD)
    suffix_scores = jnp.einsum('shjgd,sthjd->shjgt', query_rows, suffix_keys) * score_scale
    positions = lax.broadcasted_iota(jnp.int32, suffix_scores.shape, 4)
    live = positions < suffix_length.astype(jnp.int32)[:, None, None, None, None]
    suffix_scores = jnp.where(live, suffix_scores, -jnp.inf)
    suffix_out, suffix_lse = finish_piece(suffix_scores, suffix_values, 'shjgt,sthjd->shjgd')
    all_out = jnp.concatenate([block_out, suffix_out[None]], axis=0)
    all_out = lax.optimization_barrier(all_out).astype(jnp.float32)
    all_lse = jnp.concatenate([block_lse, suffix_lse[None]], axis=0)
    top = lax.optimization_barrier(jnp.max(all_lse, axis=0))
    piece_weights = jnp.exp(all_lse - top[None])
    numer = lax.optimization_barrier(jnp.sum(piece_weights[..., None] * all_out, axis=0))
    denom = lax.optimization_barrier(jnp.sum(piece_weights, axis=0))
    attention = (numer / denom[..., None]).astype(jnp.bfloat16).reshape(SAMPLES, HEAD_GROUP_COUNT * QW)
    projected = jnp.dot(attention, w_out.reshape(HEAD_GROUP_COUNT * QW, D), preferred_element_type=jnp.float32)
    state = (residual.astype(jnp.float32) + projected).astype(jnp.bfloat16)
    state_wide = lax.optimization_barrier(state).astype(jnp.float32)
    inverse_rms = lax.rsqrt(lax.optimization_barrier(jnp.mean(state_wide * state_wide, axis=1)) + EPSILON)
    scaled = (state_wide * norm_gain).astype(jnp.bfloat16)
    gate = inverse_rms[:, None] * jnp.dot(scaled, gate_matrix, preferred_element_type=jnp.float32)
    up_part = inverse_rms[:, None] * jnp.dot(scaled, w_up, preferred_element_type=jnp.float32)
    hidden = (jax.nn.silu(gate) * up_part).astype(jnp.bfloat16)
    return (state_wide + jnp.dot(hidden, w_down, preferred_element_type=jnp.float32)).astype(jnp.bfloat16)
```

```python
import functools

import jax
import jax.numpy as jnp
from jax import lax
from jax.experimental import pallas as pl
from jax.experimental.pallas import tpu as pltpu
from jax.sharding import PartitionSpec as P

D = 8192
QUERY_HEADS = 64
KEY_VALUE_HEADS = 8
HD = 128
EPSILON = 1e-05

BF16 = jnp.bfloat16
F32 = jnp.float32
VMEM_LIMIT = 48 * 1024 * 1024
STAT_ROWS = 32
LOG2E = 1.4426950408889634
LN2 = 0.6931471805599453


def params(**more):
    return pltpu.CompilerParams(vmem_limit_bytes=VMEM_LIMIT, **more)


def dot(a, b):
    return jnp.dot(a, b, preferred_element_type=F32)


def dot_nt(a, b):
    return lax.dot_general(a, b, (((1,), (1,)), ((), ())), preferred_element_type=F32)


def split3(x):
    hi = x.astype(BF16).astype(F32)
    mid = (x - hi).astype(BF16).astype(F32)
    low = (x - hi - mid).astype(BF16).astype(F32)
    return hi, mid, low


def shift(x, axis, size, k):
    return lax.ppermute(x, axis, [(i, (i + k) % size) for i in range(size)])


def attention_kernel(
    heads, chunk_ref, ids_ref, lens_ref, q_ref, pk_ref, pv_ref, sk_ref, sv_ref, msg_ref
):
    samples = q_ref.shape[0]
    rows, span = sk_ref.shape[1], sk_ref.shape[2]
    lanes_s = rows * heads
    scale2 = HD**-0.5 * LOG2E
    queries = jnp.concatenate(
        [q_ref[:, g * HD : (g + 1) * HD] for g in range(heads)], axis=0
    )

    shape = (lanes_s, heads * samples)
    lane = lax.broadcasted_iota(jnp.int32, shape, 1)
    row = lax.broadcasted_iota(jnp.int32, shape, 0)
    wanted = ids_ref[...] + lax.rem(row, heads) * samples
    pick = jnp.where(lane == wanted, 1.0, 0.0).astype(BF16)
    row_queries = dot(pick, queries)

    per_tile = min(rows, max(1, 128 // heads))
    width = per_tile * heads
    outs, lses = [], []
    for tile in range(rows // per_tile):
        at = tile * per_tile
        q_tile = row_queries[at * heads : at * heads + width]
        own = lax.broadcasted_iota(jnp.int32, (width, HD), 0) // heads
        q_wide = jnp.concatenate(
            [jnp.where(own == r, q_tile, 0.0).astype(BF16) for r in range(per_tile)], axis=1
        )
        keys = jnp.concatenate([sk_ref[0, at + r] for r in range(per_tile)], axis=1)
        s = dot_nt(keys, q_wide) * scale2
        t = lax.broadcasted_iota(jnp.int32, s.shape, 0)
        s = jnp.where(t < lens_ref[:, at * heads : at * heads + width], s, -jnp.inf)
        high = jnp.max(s, axis=0, keepdims=True)
        weights = jnp.exp2(s - high)
        total = jnp.sum(weights, axis=0, keepdims=True)
        turned = weights.T
        own_t = lax.broadcasted_iota(jnp.int32, (width, span), 0) // heads
        w_wide = jnp.concatenate(
            [jnp.where(own_t == r, turned, 0.0).astype(BF16) for r in range(per_tile)], axis=1
        )
        values = sv_ref[0, at : at + per_tile].reshape(per_tile * span, HD)
        out = dot(w_wide, values).T / total
        outs.append(out)
        lses.append(high + jnp.log2(total))
    lse_s = jnp.concatenate(lses, axis=1)
    hi, mid, low = split3(lse_s)
    sub = lax.broadcasted_iota(jnp.int32, (16, lanes_s), 0)
    stats = jnp.where(sub == 0, hi, jnp.where(sub == 1, mid, jnp.where(sub == 2, low, 1.0)))
    to_place = jnp.concatenate([jnp.concatenate(outs, axis=1), stats], axis=0).astype(BF16)
    placed = dot(to_place, pick)
    placed_lse = placed[HD : HD + 1] + placed[HD + 1 : HD + 2] + placed[HD + 2 : HD + 3]
    present = placed[HD + 3 : HD + 4]

    keys = pk_ref[0]
    values_t = pv_ref[0].T
    rows_out = []
    for g in range(heads):
        at = slice(g * samples, (g + 1) * samples)
        s = dot_nt(keys, queries[at])
        high = jnp.max(s, axis=0, keepdims=True) * scale2
        weights = jnp.exp2(s * scale2 - high)
        total = jnp.sum(weights, axis=0, keepdims=True)
        out = dot(values_t, weights.astype(BF16))
        here = present[:, at] > 0.5
        other = jnp.where(here, placed_lse[:, at], high)
        top = jnp.maximum(high, other)
        own_weight = jnp.exp2(high - top)
        other_weight = jnp.where(here, jnp.exp2(other - top), 0.0)
        both = own_weight * total + other_weight
        out = (out * own_weight + placed[:HD, at] * other_weight) / both
        msg_ref[g * HD : (g + 1) * HD, :] = out.astype(BF16)
        rows_out.append(top + jnp.log2(both))
    sub = lax.broadcasted_iota(jnp.int32, (STAT_ROWS, samples), 0)
    stats = jnp.zeros((STAT_ROWS, samples), F32)
    for g in range(heads):
        for part, value in enumerate(split3(rows_out[g])):
            stats = jnp.where(sub == part * heads + g, value, stats)
    msg_ref[heads * HD :, :] = stats.astype(BF16)


def attention_piece(chunk, kv, ids, lens, queries, prefix, suffix, heads):
    samples = queries.shape[0]
    block, rows, span = prefix.shape[1], suffix.shape[1], suffix.shape[2]
    out_rows = heads * HD + STAT_ROWS
    spec = pltpu.PrefetchScalarGridSpec(
        num_scalar_prefetch=1,
        grid=(1,),
        in_specs=[
            pl.BlockSpec(ids.shape, lambda i, c: (0, 0)),
            pl.BlockSpec(lens.shape, lambda i, c: (0, 0)),
            pl.BlockSpec((samples, heads * HD), lambda i, c: (0, c[0])),
            pl.BlockSpec((1, block, HD), lambda i, c: (0, 0, c[1])),
            pl.BlockSpec((1, block, HD), lambda i, c: (1, 0, c[1])),
            pl.BlockSpec((1, rows, span, HD), lambda i, c: (0, 0, 0, c[1])),
            pl.BlockSpec((1, rows, span, HD), lambda i, c: (1, 0, 0, c[1])),
        ],
        out_specs=pl.BlockSpec((out_rows, samples), lambda i, c: (0, 0)),
    )
    return pl.pallas_call(
        functools.partial(attention_kernel, heads),
        grid_spec=spec,
        out_shape=jax.ShapeDtypeStruct((out_rows, samples), BF16),
        compiler_params=params(),
        cost_estimate=pl.CostEstimate(
            flops=4 * samples * heads * block * HD * 4,
            bytes_accessed=2 * (2 * block + 2 * rows * span) * HD * 2,
            transcendentals=samples * heads * block,
        ),
    )(jnp.stack([chunk, kv]), ids, lens, queries, prefix, prefix, suffix, suffix)


def merge_kernel(heads, *refs):
    pieces, out_ref = refs[:-1], refs[-1]
    top_rows = heads * HD
    lses = []
    for ref in pieces:
        stats = ref[top_rows:, :].astype(F32)
        lses.append(
            stats[:heads] + stats[heads : 2 * heads] + stats[2 * heads : 3 * heads]
        )
    top = functools.reduce(jnp.maximum, lses)
    weights = [jnp.exp2(lse - top) for lse in lses]
    denom = functools.reduce(jnp.add, weights)
    weights = [w / denom for w in weights]
    for g in range(heads):
        total = None
        for ref, w in zip(pieces, weights):
            term = ref[g * HD : (g + 1) * HD, :].astype(F32) * w[g : g + 1]
            total = term if total is None else total + term
        out_ref[:, g * HD : (g + 1) * HD] = total.T.astype(BF16)


def merge(pieces, heads):
    samples = pieces[0].shape[1]
    return pl.pallas_call(
        functools.partial(merge_kernel, heads),
        out_shape=jax.ShapeDtypeStruct((samples, heads * HD), BF16),
        compiler_params=params(),
        cost_estimate=pl.CostEstimate(
            flops=2 * len(pieces) * samples * heads * HD,
            bytes_accessed=2 * (len(pieces) + 1) * samples * heads * HD,
            transcendentals=0,
        ),
    )(*pieces)


def proj_kernel(n_ctx, n_head, own_rows, n_smp, where_ref, *refs):
    attn_refs = refs[:n_smp]
    w_ref, keep_ref, *send_refs, full, lhs = refs[n_smp:]
    ctx, smp, head = where_ref[0], where_ref[1], where_ref[2]
    samples = attn_refs[0].shape[0]

    @pl.when(pl.program_id(0) == 0)
    def _():
        for k, ref in enumerate(attn_refs):
            at = lax.rem(smp + n_smp - k, n_smp) * samples
            full[pl.ds(pl.multiple_of(at, 16), samples), :] = ref[...]
        for b in range(n_head):
            h = lax.rem(head + b, n_head)
            for t in range(n_ctx):
                c = lax.rem(ctx + n_ctx - t, n_ctx)
                at = (c * n_head + h) * own_rows
                to = (b * n_ctx + t) * own_rows
                lhs[to : to + own_rows, :] = full[
                    pl.ds(pl.multiple_of(at, 16), own_rows), :
                ]

    out = dot(lhs[...], w_ref[0]).astype(BF16)
    per = n_ctx * own_rows
    keep_ref[...] = out[:per]
    for b, ref in enumerate(send_refs):
        ref[...] = out[(b + 1) * per : (b + 2) * per]


def project(where, attn, w_out, n_ctx, n_head, own_rows):
    n_smp = len(attn)
    samples, depth = attn[0].shape
    width = w_out.shape[2]
    tile = min(512, width)
    per = n_ctx * own_rows
    rows = per * n_head
    spec = pltpu.PrefetchScalarGridSpec(
        num_scalar_prefetch=1,
        grid=(width // tile,),
        in_specs=[pl.BlockSpec((samples, depth), lambda i, w: (0, 0))] * n_smp
        + [pl.BlockSpec((1, depth, tile), lambda i, w: (0, 0, i))],
        out_specs=[pl.BlockSpec((per, tile), lambda i, w: (0, i))] * n_head,
        scratch_shapes=[
            pltpu.VMEM((n_smp * samples, depth), BF16),
            pltpu.VMEM((rows, depth), BF16),
        ],
    )
    return pl.pallas_call(
        functools.partial(proj_kernel, n_ctx, n_head, own_rows, n_smp),
        grid_spec=spec,
        out_shape=[jax.ShapeDtypeStruct((per, width), BF16)] * n_head,
        compiler_params=params(),
        cost_estimate=pl.CostEstimate(
            flops=2 * rows * depth * width,
            bytes_accessed=2 * (depth * width + rows * depth + rows * width),
            transcendentals=0,
        ),
    )(where, *attn, w_out)


def exchange_heads(parts, n_head):
    total = parts[0].astype(F32)
    for b in range(1, n_head):
        total = total + shift(parts[b], "head", n_head, b).astype(F32)
    return total.astype(BF16)


def ring_sum(x, n_ctx, own_rows):
    width = x.shape[1]
    half = width // 2

    def part(t, side):
        return x[t * own_rows : (t + 1) * own_rows, side * half : (side + 1) * half]

    running = [None, None]
    for step in range(1, n_ctx):
        for side in range(2):
            t = step if side == 0 else n_ctx - step
            mine = part(t, side)
            if running[side] is not None:
                mine = (running[side].astype(F32) + mine.astype(F32)).astype(BF16)
            running[side] = shift(mine, "ctx", n_ctx, 1 if side == 0 else -1)
    return running


def state_kernel(a_ref, b_ref, own_ref, res_ref, gain_ref, state_ref, ma_ref, mb_ref):
    half = a_ref.shape[1]
    square = None
    for side, ref in enumerate((a_ref, b_ref)):
        at = slice(side * half, (side + 1) * half)
        total = (
            res_ref[:, at].astype(F32) + own_ref[:, at].astype(F32) + ref[...].astype(F32)
        )
        state = total.astype(BF16)
        state_ref[:, at] = state
        wide = state.astype(F32)
        scaled = (wide * gain_ref[:, at]).astype(BF16)
        if side == 0:
            ma_ref[...] = scaled
        else:
            mb_ref[:, :half] = scaled
        part = jnp.sum(wide * wide, axis=1, keepdims=True)
        square = part if square is None else square + part
    hi, mid, low = split3(square)
    lane = lax.broadcasted_iota(jnp.int32, (square.shape[0], HD), 1)
    stats = jnp.where(
        lane == 0, hi, jnp.where(lane == 1, mid, jnp.where(lane == 2, low, 0.0))
    )
    mb_ref[:, half:] = stats.astype(BF16)


def make_state(halves, own, residual, gain):
    rows, width = residual.shape
    return pl.pallas_call(
        state_kernel,
        out_shape=[
            jax.ShapeDtypeStruct((rows, width), BF16),
            jax.ShapeDtypeStruct((rows, width // 2), BF16),
            jax.ShapeDtypeStruct((rows, width // 2 + HD), BF16),
        ],
        compiler_params=params(),
    )(*halves, own, residual, gain)


def ring_gather(a, b, n_ctx):
    got_a, got_b = [a], [b]
    for _ in range(1, n_ctx):
        got_a.append(shift(got_a[-1], "ctx", n_ctx, 1))
        got_b.append(shift(got_b[-1], "ctx", n_ctx, -1))
    return got_a, [got_b[(n_ctx - t) % n_ctx] for t in range(n_ctx)]


def gate_up_kernel(where_ref, x_ref, g_ref, u_ref, out_ref, g_acc, u_acc):
    k = pl.program_id(0)
    x = x_ref[...]
    gate = dot(x, g_ref[...])
    up = dot(x, u_ref[...])

    @pl.when(k == 0)
    def _():
        g_acc[...] = gate
        u_acc[...] = up

    @pl.when(k > 0)
    def _():
        g_acc[...] += gate
        u_acc[...] += up

    @pl.when(k == pl.num_programs(0) - 1)
    def _():
        width = g_acc.shape[1]
        out_ref[:, :width] = g_acc[...].astype(out_ref.dtype)
        out_ref[:, width:] = u_acc[...].astype(out_ref.dtype)


def gate_up(block, x, gate_matrix, w_up, units, dtype):
    rows, depth = x.shape[0], gate_matrix.shape[0]
    tile = min(512, depth)
    spec = pltpu.PrefetchScalarGridSpec(
        num_scalar_prefetch=1,
        grid=(depth // tile,),
        in_specs=[
            pl.BlockSpec((rows, tile), lambda k, w: (0, k)),
            pl.BlockSpec((tile, units), lambda k, w: (k, w[0])),
            pl.BlockSpec((tile, units), lambda k, w: (k, w[0])),
        ],
        out_specs=pl.BlockSpec((rows, 2 * units), lambda k, w: (0, 0)),
        scratch_shapes=[pltpu.VMEM((rows, units), F32)] * 2,
    )
    return pl.pallas_call(
        gate_up_kernel,
        grid_spec=spec,
        out_shape=jax.ShapeDtypeStruct((rows, 2 * units), dtype),
        compiler_params=params(),
        cost_estimate=pl.CostEstimate(
            flops=4 * rows * depth * units,
            bytes_accessed=2 * (2 * depth * units + rows * depth + 2 * rows * units),
            transcendentals=0,
        ),
    )(block.reshape(1), x, gate_matrix, w_up)


def act_kernel(n_recv, n_sq, *refs):
    own_ref, refs = refs[0], refs[1:]
    recv, squares, out_ref = refs[:n_recv], refs[n_recv : n_recv + n_sq], refs[-1]
    total = own_ref[...].astype(F32)
    for ref in recv:
        total = total + ref[...].astype(F32)
    square = functools.reduce(jnp.add, [ref[...].astype(F32) for ref in squares])
    factor = lax.rsqrt(jnp.sum(square, axis=1, keepdims=True) / D + EPSILON)
    units = out_ref.shape[1]
    gate = factor * total[:, :units]
    up = factor * total[:, units:]
    out_ref[...] = (gate / (1.0 + jnp.exp(-gate)) * up).astype(BF16)


def activate(own, recv, squares, units):
    rows = own.shape[0]
    return pl.pallas_call(
        functools.partial(act_kernel, len(recv), len(squares)),
        out_shape=jax.ShapeDtypeStruct((rows, units), BF16),
        compiler_params=params(),
    )(own, *recv, *squares)


def down_kernel(n_parts, has_acc, n_head, where_ref, *refs):
    xs = refs[:n_parts]
    w_refs = refs[n_parts : 2 * n_parts]
    refs = refs[2 * n_parts :]
    total = None
    for x_ref, w_ref in zip(xs, w_refs):
        term = dot(x_ref[...], w_ref[...])
        total = term if total is None else total + term
    if has_acc:
        acc_ref, *outs = refs
        total = total + acc_ref[...]
        per = total.shape[0] // n_head
        for b, ref in enumerate(outs):
            ref[...] = total[b * per : (b + 1) * per].astype(BF16)
    else:
        refs[0][...] = total


def down(blocks, xs, w_down, acc, n_head):
    rows, units = xs[0].shape
    width = w_down.shape[1]
    tile = min(512, width)
    n = len(xs)

    def w_spec(i):
        return pl.BlockSpec((units, tile), lambda k, w: (w[i], k))

    in_specs = [pl.BlockSpec((rows, units), lambda k, w: (0, 0))] * n
    in_specs += [w_spec(i) for i in range(n)]
    args = [*xs, *([w_down] * n)]
    if acc is not None:
        in_specs.append(pl.BlockSpec((rows, tile), lambda k, w: (0, k)))
        args.append(acc)
        per = rows // n_head
        out_shape = [jax.ShapeDtypeStruct((per, width), BF16)] * n_head
        out_specs = [pl.BlockSpec((per, tile), lambda k, w: (0, k))] * n_head
    else:
        out_shape = jax.ShapeDtypeStruct((rows, width), F32)
        out_specs = pl.BlockSpec((rows, tile), lambda k, w: (0, k))
    return pl.pallas_call(
        functools.partial(down_kernel, n, acc is not None, n_head),
        grid_spec=pltpu.PrefetchScalarGridSpec(
            num_scalar_prefetch=1,
            grid=(width // tile,),
            in_specs=in_specs,
            out_specs=out_specs,
        ),
        out_shape=out_shape,
        compiler_params=params(),
        cost_estimate=pl.CostEstimate(
            flops=2 * rows * units * n * width,
            bytes_accessed=2 * units * n * width + 6 * rows * width,
            transcendentals=0,
        ),
    )(jnp.stack(blocks), *args)


def on_device(
    n_ctx,
    n_smp,
    n_head,
    queries,
    prefix_cache,
    suffix_cache,
    suffix_length,
    cache_sample,
    residual,
    w_out,
    norm_gain,
    gate_matrix,
    w_up,
    w_down,
):
    ctx, smp, head = (lax.axis_index(name) for name in ("ctx", "smp", "head"))
    samples = queries.shape[0]
    own_rows = residual.shape[0]
    queries = queries.reshape(samples, -1)
    prefix = prefix_cache.reshape(2, prefix_cache.shape[1], -1)
    rows, span = suffix_cache.shape[1:3]
    suffix = suffix_cache.reshape(2, rows, span, -1)
    kv_heads = prefix.shape[2] // HD
    group = QUERY_HEADS // KEY_VALUE_HEADS
    heads = kv_heads * group // n_ctx

    row_ids = lax.dynamic_slice_in_dim(cache_sample, (ctx * n_smp + smp) * rows, rows, 0)
    local_ids = row_ids % samples
    ids = jnp.repeat(local_ids, heads)[:, None]
    one_hot = local_ids[:, None] == jnp.arange(samples, dtype=jnp.int32)[None, :]
    row_lengths = jnp.sum(jnp.where(one_hot, suffix_length[None, :], 0), axis=1)
    lens = jnp.repeat(row_lengths, heads)[None, :]

    order = sorted(range(1, n_ctx), key=lambda k: -min(k, n_ctx - k)) + [0]
    pieces = []
    for k in order:
        chunk = (ctx + k) % n_ctx
        kv = chunk * heads // group
        piece = attention_piece(chunk, kv, ids, lens, queries, prefix, suffix, heads)
        pieces.append(shift(piece, "ctx", n_ctx, k) if k else piece)
    attn = merge(pieces, heads)
    gathered = [attn] + [shift(attn, "smp", n_smp, k) for k in range(1, n_smp)]

    where = jnp.stack([ctx, smp, head])
    parts = project(where, gathered, w_out, n_ctx, n_head, own_rows)
    partial = exchange_heads(parts, n_head)
    halves = ring_sum(partial, n_ctx, own_rows)
    state, msg_a, msg_b = make_state(halves, partial[:own_rows], residual, norm_gain[None, :])

    got_a, got_b = ring_gather(msg_a, msg_b, n_ctx)
    left = jnp.concatenate(got_a, axis=0)
    right = jnp.concatenate(got_b, axis=0)
    full = jnp.concatenate([left, right], axis=1)
    full = jnp.concatenate(
        [full] + [shift(full, "head", n_head, b) for b in range(1, n_head)], axis=0
    )
    depth = gate_matrix.shape[0]
    square = full[:, depth:]
    squares = [square] + [shift(square, "smp", n_smp, k) for k in range(1, n_smp)]

    share = gate_matrix.shape[1] // n_smp
    splits = min(2, share // 128)
    units = share // splits
    received = [[] for _ in range(splits)]
    for k in range(1, n_smp):
        for q in range(splits):
            block = (smp + k) % n_smp * splits + q
            msg = gate_up(block, full, gate_matrix, w_up, units, BF16)
            received[q].append(shift(msg, "smp", n_smp, k))
    own = [
        gate_up(smp * splits + q, full, gate_matrix, w_up, units, F32) for q in range(splits)
    ]
    hidden, others = [], []
    for q in range(splits):
        hidden.append(activate(own[q], received[q], squares, units))
        others.append([shift(hidden[q], "smp", n_smp, k) for k in range(1, n_smp)])
    acc = down([smp * splits + q for q in range(splits)], hidden, w_down, None, n_head)
    blocks, xs = [], []
    for k in range(1, n_smp):
        for q in range(splits):
            blocks.append((smp + n_smp - k) % n_smp * splits + q)
            xs.append(others[q][k - 1])
    parts = down(blocks, xs, w_down, acc, n_head)
    partial = exchange_heads(parts, n_head)
    halves = ring_sum(partial, n_ctx, own_rows)
    total = (
        jnp.concatenate(halves, axis=1).astype(F32)
        + partial[:own_rows].astype(F32)
        + state.astype(F32)
    )
    return total.astype(BF16)


def solution(mesh):
    in_specs = (
        P(("group", "smp"), "head", None),
        P(None, ("group", "ctx"), "head", None),
        P(None, ("group", "ctx", "smp"), None, "head", None),
        P(("group", "smp")),
        P("group"),
        P(("group", "ctx", "head"), "smp"),
        P("head", "ctx", "smp"),
        P("smp"),
        P("smp", ("ctx", "head")),
        P("smp", ("ctx", "head")),
        P(("ctx", "head"), "smp"),
    )
    out_specs = P(("group", "ctx", "head"), "smp")
    body = functools.partial(
        on_device, mesh.shape["ctx"], mesh.shape["smp"], mesh.shape["head"]
    )
    return jax.shard_map(
        body, mesh=mesh, in_specs=in_specs, out_specs=out_specs, check_vma=False
    )
```

```python
import functools

import jax
import jax.numpy as jnp
from jax import lax
from jax.experimental import pallas as pl
from jax.experimental.pallas import tpu as pltpu
from jax.sharding import PartitionSpec as P

D = 8192
QUERY_HEADS = 64
KEY_VALUE_HEADS = 8
HD = 128
EPSILON = 1e-05

BF16 = jnp.bfloat16
F32 = jnp.float32
VMEM_LIMIT = 48 * 1024 * 1024
STAT_ROWS = 32
PIECES = 4
LOG2E = 1.4426950408889634
LN2 = 0.6931471805599453


def params(limit=VMEM_LIMIT):
    return pltpu.CompilerParams(vmem_limit_bytes=limit)


def cost(us):
    return pl.CostEstimate(
        flops=int(us * 1.1e9), bytes_accessed=int(us * 3.6e6), transcendentals=0
    )


IN_PLACE = pl.BlockSpec(memory_space=pl.ANY)
WHOLE = pl.BlockSpec(memory_space=pltpu.VMEM)
SCALARS = pl.BlockSpec(memory_space=pltpu.SMEM)


def run(name, kernel, in_specs, args, after=(), **more):
    n, m = len(args), len(after)

    def body(*refs):
        return kernel(*refs[:n], *refs[n + m :])

    return pl.pallas_call(
        body,
        name=name,
        in_specs=list(in_specs) + [IN_PLACE] * m,
        compiler_params=params(),
        **{"cost_estimate": cost(0.2), **more},
    )(*args, *after)


def dot(a, b):
    return jnp.dot(a, b, preferred_element_type=F32)


def dot_nt(a, b):
    return lax.dot_general(a, b, (((1,), (1,)), ((), ())), preferred_element_type=F32)


def split3(x):
    hi = x.astype(BF16).astype(F32)
    mid = (x - hi).astype(BF16).astype(F32)
    low = (x - hi - mid).astype(BF16).astype(F32)
    return hi, mid, low


def shift(x, axis, size, k):
    return lax.ppermute(x, axis, [(i, (i + k) % size) for i in range(size)])


def attention_kernel(
    heads, chunk_ref, ids_ref, lens_ref, q_ref, pk_ref, pv_ref, sk_ref, sv_ref, msg_ref
):
    samples = q_ref.shape[0]
    rows, span = sk_ref.shape[1], sk_ref.shape[2]
    lanes_s = rows * heads
    scale2 = HD**-0.5 * LOG2E
    queries = jnp.concatenate(
        [q_ref[:, g * HD : (g + 1) * HD] for g in range(heads)], axis=0
    )

    shape = (lanes_s, heads * samples)
    lane = lax.broadcasted_iota(jnp.int32, shape, 1)
    row = lax.broadcasted_iota(jnp.int32, shape, 0)
    wanted = ids_ref[...] + lax.rem(row, heads) * samples
    pick = jnp.where(lane == wanted, 1.0, 0.0).astype(BF16)
    row_queries = dot(pick, queries)

    per_tile = min(rows, max(1, 128 // heads))
    width = per_tile * heads
    outs, lses = [], []
    for tile in range(rows // per_tile):
        at = tile * per_tile
        q_tile = row_queries[at * heads : at * heads + width]
        own = lax.broadcasted_iota(jnp.int32, (width, HD), 0) // heads
        q_wide = jnp.concatenate(
            [jnp.where(own == r, q_tile, 0.0).astype(BF16) for r in range(per_tile)], axis=1
        )
        keys = jnp.concatenate([sk_ref[0, at + r] for r in range(per_tile)], axis=1)
        s = dot_nt(keys, q_wide) * scale2
        t = lax.broadcasted_iota(jnp.int32, s.shape, 0)
        s = jnp.where(t < lens_ref[:, at * heads : at * heads + width], s, -jnp.inf)
        high = jnp.max(s, axis=0, keepdims=True)
        weights = jnp.exp2(s - high)
        total = jnp.sum(weights, axis=0, keepdims=True)
        turned = weights.T
        own_t = lax.broadcasted_iota(jnp.int32, (width, span), 0) // heads
        w_wide = jnp.concatenate(
            [jnp.where(own_t == r, turned, 0.0).astype(BF16) for r in range(per_tile)], axis=1
        )
        values = sv_ref[0, at : at + per_tile].reshape(per_tile * span, HD)
        out = dot(w_wide, values).T / total
        outs.append(out)
        lses.append(high + jnp.log2(total))
    lse_s = jnp.concatenate(lses, axis=1)
    hi, mid, low = split3(lse_s)
    sub = lax.broadcasted_iota(jnp.int32, (16, lanes_s), 0)
    stats = jnp.where(sub == 0, hi, jnp.where(sub == 1, mid, jnp.where(sub == 2, low, 1.0)))
    to_place = jnp.concatenate([jnp.concatenate(outs, axis=1), stats], axis=0).astype(BF16)
    placed = dot(to_place, pick)
    placed_lse = placed[HD : HD + 1] + placed[HD + 1 : HD + 2] + placed[HD + 2 : HD + 3]
    present = placed[HD + 3 : HD + 4]

    keys = pk_ref[0]
    values_t = pv_ref[0].T
    rows_out = []
    for g in range(heads):
        at = slice(g * samples, (g + 1) * samples)
        s = dot_nt(keys, queries[at])
        high = jnp.max(s, axis=0, keepdims=True) * scale2
        weights = jnp.exp2(s * scale2 - high)
        total = jnp.sum(weights, axis=0, keepdims=True)
        out = dot(values_t, weights.astype(BF16))
        here = present[:, at] > 0.5
        other = jnp.where(here, placed_lse[:, at], high)
        top = jnp.maximum(high, other)
        own_weight = jnp.exp2(high - top)
        other_weight = jnp.where(here, jnp.exp2(other - top), 0.0)
        both = own_weight * total + other_weight
        out = out * (own_weight / both) + placed[:HD, at] * (other_weight / both)
        msg_ref[g * HD : (g + 1) * HD, :] = out.astype(BF16)
        rows_out.append(top + jnp.log2(both))
    sub = lax.broadcasted_iota(jnp.int32, (STAT_ROWS, samples), 0)
    stats = jnp.zeros((STAT_ROWS, samples), F32)
    for g in range(heads):
        for part, value in enumerate(split3(rows_out[g])):
            stats = jnp.where(sub == part * heads + g, value, stats)
    msg_ref[heads * HD :, :] = stats.astype(BF16)


def attention_piece(chunk, kv, ids, lens, queries, prefix, suffix, heads):
    samples = queries.shape[0]
    block, rows, span = prefix.shape[1], suffix.shape[1], suffix.shape[2]
    out_rows = heads * HD + STAT_ROWS
    spec = pltpu.PrefetchScalarGridSpec(
        num_scalar_prefetch=1,
        grid=(1,),
        in_specs=[
            pl.BlockSpec(ids.shape, lambda i, c: (0, 0)),
            pl.BlockSpec(lens.shape, lambda i, c: (0, 0)),
            pl.BlockSpec((samples, heads * HD), lambda i, c: (0, c[0])),
            pl.BlockSpec((1, block, HD), lambda i, c: (0, 0, c[1])),
            pl.BlockSpec((1, block, HD), lambda i, c: (1, 0, c[1])),
            pl.BlockSpec((1, rows, span, HD), lambda i, c: (0, 0, 0, c[1])),
            pl.BlockSpec((1, rows, span, HD), lambda i, c: (1, 0, 0, c[1])),
        ],
        out_specs=pl.BlockSpec((out_rows, samples), lambda i, c: (0, 0)),
    )
    return pl.pallas_call(
        functools.partial(attention_kernel, heads),
        grid_spec=spec,
        out_shape=jax.ShapeDtypeStruct((out_rows, samples), BF16),
        compiler_params=params(),
        cost_estimate=cost(6),
    )(jnp.stack([chunk, kv]), ids, lens, queries, prefix, prefix, suffix, suffix)


def merge_kernel(heads, *refs):
    pieces, out_ref = refs[:-1], refs[-1]
    top_rows = heads * HD
    lses = []
    for ref in pieces:
        stats = ref[top_rows:, :].astype(F32)
        lses.append(
            stats[:heads] + stats[heads : 2 * heads] + stats[2 * heads : 3 * heads]
        )
    top = functools.reduce(jnp.maximum, lses)
    weights = [jnp.exp2(lse - top) for lse in lses]
    denom = functools.reduce(jnp.add, weights)
    weights = [w / denom for w in weights]
    for g in range(heads):
        total = None
        for ref, w in zip(pieces, weights):
            term = ref[g * HD : (g + 1) * HD, :].astype(F32) * w[g : g + 1]
            total = term if total is None else total + term
        out_ref[:, g * HD : (g + 1) * HD] = total.T.astype(BF16)


def merge(pieces, heads):
    samples = pieces[0].shape[1]
    return run(
        "merge",
        functools.partial(merge_kernel, heads),
        [WHOLE] * len(pieces),
        pieces,
        out_specs=WHOLE,
        out_shape=jax.ShapeDtypeStruct((samples, heads * HD), BF16),
        cost_estimate=cost(1.3),
    )


def proj_kernel(n_ctx, n_head, own_rows, n_smp, parts, chunks, where_ref, *refs):
    attn_refs, w_hbm, refs = refs[:n_smp], refs[n_smp], refs[n_smp + 1 :]
    out_refs, (full, lhs, w_buf, sems) = refs[:-4], refs[-4:]
    ctx, smp, head = where_ref[0], where_ref[1], where_ref[2]
    samples = attn_refs[0].shape[0]
    tile = w_buf.shape[2]
    copies = [
        pltpu.make_async_copy(
            w_hbm.at[0, :, pl.ds(i * tile, tile)], w_buf.at[i], sems.at[i]
        )
        for i in range(chunks)
    ]
    for copy in copies:
        copy.start()
    for k, ref in enumerate(attn_refs):
        at = lax.rem(smp + n_smp - k, n_smp) * samples
        full[pl.ds(pl.multiple_of(at, 16), samples), :] = ref[...]
    step = own_rows // parts
    to = 0
    for p in range(parts):
        for b in range(n_head):
            h = lax.rem(head + b, n_head)
            for t in range(n_ctx):
                c = lax.rem(ctx + n_ctx - t, n_ctx)
                at = (c * n_head + h) * own_rows + p * step
                lhs[to : to + step, :] = full[pl.ds(pl.multiple_of(at, step), step), :]
                to += step
    per = n_ctx * step
    for i, copy in enumerate(copies):
        copy.wait()
        out = dot(lhs[...], w_buf[i]).astype(BF16)
        for j, ref in enumerate(out_refs):
            ref[:, i * tile : (i + 1) * tile] = out[j * per : (j + 1) * per]


def project(where, attn, w_out, n_ctx, n_head, own_rows, parts):
    n_smp = len(attn)
    samples, depth = attn[0].shape
    width = w_out.shape[2]
    chunks = 4
    tile = width // chunks
    per = n_ctx * own_rows // parts
    rows = per * parts * n_head
    return run(
        "project",
        functools.partial(proj_kernel, n_ctx, n_head, own_rows, n_smp, parts, chunks),
        [SCALARS] + [WHOLE] * n_smp + [IN_PLACE],
        [where, *attn, w_out],
        out_specs=[WHOLE] * (n_head * parts),
        out_shape=[jax.ShapeDtypeStruct((per, width), BF16)] * (n_head * parts),
        scratch_shapes=[
            pltpu.VMEM((n_smp * samples, depth), BF16),
            pltpu.VMEM((rows, depth), BF16),
            pltpu.VMEM((chunks, depth, tile), BF16),
            pltpu.SemaphoreType.DMA((chunks,)),
        ],
        cost_estimate=cost(5),
    )


def add_heads_kernel(n_ctx, keep_ref, *refs):
    recv, outs = refs[:-n_ctx], refs[-n_ctx:]
    rows = outs[0].shape[0]
    n_pieces = outs[0].shape[1] // recv[0].shape[1]
    width = recv[0].shape[1]
    for t, ref in enumerate(outs):
        at = slice(t * rows, (t + 1) * rows)
        for j in range(n_pieces):
            columns = slice(j * width, (j + 1) * width)
            total = keep_ref[at, columns].astype(F32)
            for other in recv[j::n_pieces]:
                total = total + other[at].astype(F32)
            ref[:, columns] = total.astype(BF16)


def exchange_heads(by_head, n_ctx, pieces, after=()):
    rows, width = by_head[0].shape
    n_head = len(by_head)
    step = width // pieces
    recv = [
        shift(by_head[b][:, j * step : (j + 1) * step], "head", n_head, b)
        for b in range(1, n_head)
        for j in range(pieces)
    ]
    return run(
        "add_heads",
        functools.partial(add_heads_kernel, n_ctx),
        [WHOLE] * (1 + len(recv)),
        [by_head[0], *recv],
        after,
        out_specs=[WHOLE] * n_ctx,
        out_shape=[jax.ShapeDtypeStruct((rows // n_ctx, width), BF16)] * n_ctx,
    )


def far_first(n):
    return sorted(range(1, n), key=lambda k: -min(k, n - k))


def send_sums(sums):
    n_ctx = len(sums)
    return [sums[0]] + [shift(sums[t], "ctx", n_ctx, -t) for t in far_first(n_ctx)]


def send_rows(x, n_ctx):
    got = {t: shift(x, "ctx", n_ctx, t) for t in far_first(n_ctx)}
    return [x] + [got[t] for t in range(1, n_ctx)]


def join_kernel(*refs):
    pieces, out_ref = refs[:-1], refs[-1]
    rows = pieces[0].shape[0]
    for t, ref in enumerate(pieces):
        out_ref[t * rows : (t + 1) * rows, :] = ref[...]


def join(pieces, after):
    rows, width = pieces[0].shape
    return run(
        "join",
        join_kernel,
        [WHOLE] * len(pieces),
        pieces,
        after,
        out_specs=WHOLE,
        out_shape=jax.ShapeDtypeStruct((rows * len(pieces), width), BF16),
    )


def state_kernel(n_pieces, *refs):
    pieces, (res_ref, gain_ref, state_ref, msg_ref) = refs[:n_pieces], refs[n_pieces:]
    width = res_ref.shape[1]
    total = res_ref[...].astype(F32)
    for ref in pieces:
        total = total + ref[...].astype(F32)
    state = total.astype(BF16)
    state_ref[...] = state
    wide = state.astype(F32)
    msg_ref[:, :width] = (wide * gain_ref[...]).astype(BF16)
    hi, mid, low = split3(jnp.sum(wide * wide, axis=1, keepdims=True))
    lane = lax.broadcasted_iota(jnp.int32, (hi.shape[0], HD), 1)
    stats = jnp.where(
        lane == 0, hi, jnp.where(lane == 1, mid, jnp.where(lane == 2, low, 0.0))
    )
    msg_ref[:, width:] = stats.astype(BF16)


def make_state(pieces, residual, gain, after):
    rows, width = residual.shape
    return run(
        "state",
        functools.partial(state_kernel, len(pieces)),
        [WHOLE] * (len(pieces) + 2),
        [*pieces, residual, gain],
        after,
        out_specs=[WHOLE] * 2,
        out_shape=[
            jax.ShapeDtypeStruct((rows, width), BF16),
            jax.ShapeDtypeStruct((rows, width + HD), BF16),
        ],
    )


def finish_kernel(*refs):
    total = refs[0][...].astype(F32)
    for ref in refs[1:-1]:
        total = total + ref[...].astype(F32)
    refs[-1][...] = total.astype(refs[-1].dtype)


def finish(pieces):
    def add(terms, dtype):
        return run(
            "finish",
            finish_kernel,
            [WHOLE] * len(terms),
            terms,
            out_specs=WHOLE,
            out_shape=jax.ShapeDtypeStruct(terms[0].shape, dtype),
        )

    return add([add(pieces[1:], F32), pieces[0]], BF16)


def gate_up_kernel(chunks, n_parts, where_ref, *refs):
    parts, (g_hbm, u_hbm, out_ref, x, g_buf, u_buf, g_sem, u_sem) = (
        refs[:n_parts],
        refs[n_parts:],
    )
    tile, units = g_buf.shape[1:]
    at = pl.multiple_of(where_ref[0] * units, 128)
    copies = []
    for i in range(chunks):
        block = (pl.ds(i * tile, tile), pl.ds(at, units))
        for hbm, buf, sem in ((g_hbm, g_buf, g_sem), (u_hbm, u_buf, u_sem)):
            copies.append(pltpu.make_async_copy(hbm.at[block], buf.at[i], sem.at[i]))
    for copy in copies:
        copy.start()
    row = 0
    for ref in parts:
        x[row : row + ref.shape[0]] = ref[:, : x.shape[1]]
        row += ref.shape[0]
    gate = up = None
    for i in range(chunks):
        lhs = x[:, i * tile : (i + 1) * tile]
        copies[2 * i].wait()
        term = dot(lhs, g_buf[i])
        gate = term if gate is None else gate + term
        copies[2 * i + 1].wait()
        term = dot(lhs, u_buf[i])
        up = term if up is None else up + term
    out_ref[:, :units] = gate.astype(out_ref.dtype)
    out_ref[:, units : 2 * units] = up.astype(out_ref.dtype)
    row = 0
    for ref in parts:
        out_ref[row : row + ref.shape[0], 2 * units :] = ref[:, x.shape[1] :].astype(
            out_ref.dtype
        )
        row += ref.shape[0]


def gate_up(block, parts, gate_matrix, w_up, units, dtype, after=()):
    rows, depth = sum(p.shape[0] for p in parts), gate_matrix.shape[0]
    chunks = 8
    tile = depth // chunks
    return run(
        "gate_up",
        functools.partial(gate_up_kernel, chunks, len(parts)),
        [SCALARS] + [WHOLE] * len(parts) + [IN_PLACE] * 2,
        [block.reshape(1), *parts, gate_matrix, w_up],
        after,
        out_specs=WHOLE,
        out_shape=jax.ShapeDtypeStruct((rows, 2 * units + HD), dtype),
        scratch_shapes=[pltpu.VMEM((rows, depth), BF16)]
        + [pltpu.VMEM((chunks, tile, units), BF16)] * 2
        + [pltpu.SemaphoreType.DMA((chunks,))] * 2,
        cost_estimate=cost(2 + 4.2 * units / 1024),
    )


def act_kernel(own_ref, *refs):
    recv, out_ref = refs[:-1], refs[-1]
    total = own_ref[...]
    for ref in recv:
        total = total + ref[...].astype(F32)
    units = out_ref.shape[1]
    square = jnp.sum(total[:, 2 * units :], axis=1, keepdims=True)
    factor = lax.rsqrt(square / D + EPSILON)
    gate = factor * total[:, :units]
    up = factor * total[:, units : 2 * units]
    out_ref[...] = (gate / (1.0 + jnp.exp(-gate)) * up).astype(BF16)


def activate(own, recv, units, after):
    return run(
        "activate",
        act_kernel,
        [WHOLE] * (1 + len(recv)),
        [own, *recv],
        after,
        out_specs=WHOLE,
        out_shape=jax.ShapeDtypeStruct((own.shape[0], units), BF16),
    )


def down_kernel(n_parts, chunks, has_acc, last, n_head, where_ref, *refs):
    xs, refs = refs[:n_parts], refs[n_parts:]
    if has_acc:
        acc_ref, w_hbm, *outs, w_buf, sems = refs
    else:
        w_hbm, *outs, w_buf, sems = refs
    units, tile = w_buf.shape[2:]
    copies = []
    for i in range(chunks):
        for p in range(n_parts):
            at = pl.multiple_of(where_ref[p] * units, 16)
            copies.append(
                pltpu.make_async_copy(
                    w_hbm.at[pl.ds(at, units), pl.ds(i * tile, tile)],
                    w_buf.at[i, p],
                    sems.at[i, p],
                )
            )
    for copy in copies:
        copy.start()
    for i in range(chunks):
        total = acc_ref[:, i * tile : (i + 1) * tile] if has_acc else None
        for p in range(n_parts):
            copies[i * n_parts + p].wait()
            term = dot(xs[p][...], w_buf[i, p])
            total = term if total is None else total + term
        if last:
            per = total.shape[0] // n_head
            for b in range(n_head):
                outs[b][:, i * tile : (i + 1) * tile] = total[
                    b * per : (b + 1) * per
                ].astype(BF16)
        else:
            outs[0][:, i * tile : (i + 1) * tile] = total


def down(blocks, xs, w_down, acc, last, n_head, after):
    rows, units = xs[0].shape
    width = w_down.shape[1]
    chunks = 4
    tile = width // chunks
    n = len(xs)
    args = list(xs) + ([] if acc is None else [acc])
    if last:
        out_shape = [jax.ShapeDtypeStruct((rows // n_head, width), BF16)] * n_head
    else:
        out_shape = [jax.ShapeDtypeStruct((rows, width), F32)]
    out = run(
        "down",
        functools.partial(down_kernel, n, chunks, acc is not None, last, n_head),
        [SCALARS] + [WHOLE] * len(args) + [IN_PLACE],
        [jnp.stack(blocks), *args, w_down],
        after,
        out_specs=[WHOLE] * len(out_shape),
        out_shape=out_shape,
        scratch_shapes=[
            pltpu.VMEM((chunks, n, units, tile), BF16),
            pltpu.SemaphoreType.DMA((chunks, n)),
        ],
        cost_estimate=cost(4 * n),
    )
    return out if last else out[0]


def on_device(
    n_ctx,
    n_smp,
    n_head,
    queries,
    prefix_cache,
    suffix_cache,
    suffix_length,
    cache_sample,
    residual,
    w_out,
    norm_gain,
    gate_matrix,
    w_up,
    w_down,
):
    ctx, smp, head = (lax.axis_index(name) for name in ("ctx", "smp", "head"))
    samples = queries.shape[0]
    own_rows = residual.shape[0]
    queries = queries.reshape(samples, -1)
    prefix = prefix_cache.reshape(2, prefix_cache.shape[1], -1)
    rows, span = suffix_cache.shape[1:3]
    suffix = suffix_cache.reshape(2, rows, span, -1)
    kv_heads = prefix.shape[2] // HD
    group = QUERY_HEADS // KEY_VALUE_HEADS
    heads = kv_heads * group // n_ctx

    row_ids = lax.dynamic_slice_in_dim(cache_sample, (ctx * n_smp + smp) * rows, rows, 0)
    local_ids = row_ids % samples
    ids = jnp.repeat(local_ids, heads)[:, None]
    one_hot = local_ids[:, None] == jnp.arange(samples, dtype=jnp.int32)[None, :]
    row_lengths = jnp.sum(jnp.where(one_hot, suffix_length[None, :], 0), axis=1)
    lens = jnp.repeat(row_lengths, heads)[None, :]

    pieces = []
    for k in far_first(n_ctx) + [0]:
        chunk = (ctx + k) % n_ctx
        kv = chunk * heads // group
        piece = attention_piece(chunk, kv, ids, lens, queries, prefix, suffix, heads)
        pieces.append(shift(piece, "ctx", n_ctx, k) if k else piece)

    parts = 2 if own_rows % 32 == 0 else 1
    step = own_rows // parts
    where = jnp.stack([ctx, smp, head])
    every = range(parts)
    others = range(1, n_smp)
    attn = merge(pieces, heads)
    gathered = [attn] + [shift(attn, "smp", n_smp, k) for k in others]
    by_head = project(where, gathered, w_out, n_ctx, n_head, own_rows, parts)
    by_head = [by_head[p * n_head : (p + 1) * n_head] for p in every]
    all_sums = [exchange_heads(by_head[p], n_ctx, 1) for p in every]
    units = gate_matrix.shape[1] // n_smp
    states, rows, full = [None] * parts, [None] * parts, [None] * parts
    received, own, hidden, theirs = ([None] * parts for _ in range(4))
    sums = [None] * parts
    done = []

    def state_step(p):
        nonlocal done
        states[p], message = make_state(
            send_sums(all_sums[p]), residual[p * step : (p + 1) * step], gain, done
        )
        rows[p] = send_rows(message, n_ctx)
        done = [states[p]]

    def others_step(p):
        nonlocal done
        joined = join(rows[p], done)
        full[p] = [shift(joined, "head", n_head, b) if b else joined for b in range(n_head)]
        received[p] = []
        for k in others:
            block = (smp + k) % n_smp
            send = gate_up(block, full[p], gate_matrix, w_up, units, BF16, done)
            done = [send]
            received[p].append(shift(send, "smp", n_smp, k))

    def own_step(p):
        nonlocal done
        own[p] = gate_up(smp, full[p], gate_matrix, w_up, units, F32, done)
        done = [own[p]]

    def hidden_step(p):
        nonlocal done
        hidden[p] = activate(own[p], received[p], units, done)
        theirs[p] = [shift(hidden[p], "smp", n_smp, k) for k in others]
        done = [hidden[p]]

    blocks = [(smp + n_smp - k) % n_smp for k in range(n_smp)]

    def down_step(p, first, count, acc):
        nonlocal done
        xs = [hidden[p], *theirs[p]][first : first + count]
        last = first + count == n_smp
        out = down(blocks[first : first + count], xs, w_down, acc, last, n_head, done)
        done = [out[0] if last else out]
        return out

    gain = norm_gain[None, :]
    state_step(0)
    for p in every:
        others_step(p)
        if p + 1 < parts:
            state_step(p + 1)
            own_step(p)
            hidden_step(p)
            continue
        own_step(p)
        for q in range(p):
            sums[q] = exchange_heads(down_step(q, 0, n_smp, None), n_ctx, PIECES)
        hidden_step(p)
        acc = down_step(p, 0, 1, None)
        by_head = down_step(p, 1, n_smp - 1, acc)
    outs = []
    for p in range(parts - 1):
        outs.append(finish([states[p], *send_sums(sums[p])]))
    sums[-1] = exchange_heads(by_head, n_ctx, PIECES, outs)
    outs.append(finish([states[-1], *send_sums(sums[-1])]))
    return jnp.concatenate(outs, axis=0)


def solution(mesh):
    in_specs = (
        P(("group", "smp"), "head", None),
        P(None, ("group", "ctx"), "head", None),
        P(None, ("group", "ctx", "smp"), None, "head", None),
        P(("group", "smp")),
        P("group"),
        P(("group", "ctx", "head"), "smp"),
        P("head", "ctx", "smp"),
        P("smp"),
        P("smp", ("ctx", "head")),
        P("smp", ("ctx", "head")),
        P(("ctx", "head"), "smp"),
    )
    out_specs = P(("group", "ctx", "head"), "smp")
    body = functools.partial(
        on_device, mesh.shape["ctx"], mesh.shape["smp"], mesh.shape["head"]
    )
    return jax.shard_map(
        body, mesh=mesh, in_specs=in_specs, out_specs=out_specs, check_vma=False
    )
```

```python
import functools

import jax
import jax.numpy as jnp
from jax import lax
from jax.experimental import pallas as pl
from jax.experimental.pallas import tpu as pltpu
from jax.sharding import PartitionSpec as P

D = 8192
QUERY_HEADS = 64
KEY_VALUE_HEADS = 8
HD = 128
EPSILON = 1e-05

BF16 = jnp.bfloat16
F32 = jnp.float32
VMEM_LIMIT = 48 * 1024 * 1024
STAT_ROWS = 32
PIECES = 1
LOG2E = 1.4426950408889634
LN2 = 0.6931471805599453


def params(limit=VMEM_LIMIT):
    return pltpu.CompilerParams(vmem_limit_bytes=limit)


def cost(us):
    return pl.CostEstimate(
        flops=int(us * 1.1e9), bytes_accessed=int(us * 3.6e6), transcendentals=0
    )


IN_PLACE = pl.BlockSpec(memory_space=pl.ANY)
WHOLE = pl.BlockSpec(memory_space=pltpu.VMEM)
SCALARS = pl.BlockSpec(memory_space=pltpu.SMEM)


def run(name, kernel, in_specs, args, after=(), limit=VMEM_LIMIT, **more):
    n, m = len(args), len(after)

    def body(*refs):
        return kernel(*refs[:n], *refs[n + m :])

    return pl.pallas_call(
        body,
        name=name,
        in_specs=list(in_specs) + [IN_PLACE] * m,
        compiler_params=params(limit),
        **{"cost_estimate": cost(0.2), **more},
    )(*args, *after)


def dot(a, b):
    return jnp.dot(a, b, preferred_element_type=F32)


def dot_nt(a, b):
    return lax.dot_general(a, b, (((1,), (1,)), ((), ())), preferred_element_type=F32)


def split3(x):
    hi = x.astype(BF16).astype(F32)
    mid = (x - hi).astype(BF16).astype(F32)
    low = (x - hi - mid).astype(BF16).astype(F32)
    return hi, mid, low


def shift(x, axis, size, k):
    return lax.ppermute(x, axis, [(i, (i + k) % size) for i in range(size)])


def attention_kernel(
    heads,
    groups,
    where_ref,
    sample_hbm,
    length_hbm,
    q_hbm,
    prefix_hbm,
    suffix_hbm,
    msg_ref,
    sample_ref,
    length_ref,
    q_ref,
    prefix_ref,
    suffix_ref,
    number_sems,
    sems,
):
    samples = q_ref.shape[0]
    rows, span = suffix_ref.shape[1:3]
    lanes_s = rows * heads
    scale2 = HD**-0.5 * LOG2E
    q_at = pl.ds(pl.multiple_of(where_ref[0] * (heads * HD), HD), heads * HD)
    kv_at = pl.ds(pl.multiple_of(where_ref[1] * HD, HD), HD)
    numbers = [
        pltpu.make_async_copy(sample_hbm, sample_ref, number_sems.at[0]),
        pltpu.make_async_copy(length_hbm, length_ref, number_sems.at[1]),
    ]
    early = [
        pltpu.make_async_copy(q_hbm.at[:, q_at], q_ref, sems.at[0]),
        pltpu.make_async_copy(prefix_hbm.at[0, :, kv_at], prefix_ref.at[0], sems.at[1]),
        pltpu.make_async_copy(prefix_hbm.at[1, :, kv_at], prefix_ref.at[1], sems.at[2]),
    ]
    late = []
    some = rows // groups
    for which in range(2):
        for g in range(groups):
            part = pl.ds(g * some, some)
            late.append(
                pltpu.make_async_copy(
                    suffix_hbm.at[which, part, :, kv_at],
                    suffix_ref.at[which, part],
                    sems.at[3 + which * groups + g],
                )
            )
    for copy in numbers + early + late:
        copy.start()

    for copy in numbers:
        copy.wait()
    column = lax.broadcasted_iota(jnp.int32, (lanes_s, 1), 0) // heads
    across = lax.broadcasted_iota(jnp.int32, (1, lanes_s), 1) // heads
    ids = jnp.zeros((lanes_s, 1), jnp.int32)
    lens = jnp.zeros((1, lanes_s), jnp.int32)
    for r in range(rows):
        sample = lax.rem(sample_ref[where_ref[2] + r], samples)
        ids = jnp.where(column == r, sample, ids)
        lens = jnp.where(across == r, length_ref[sample], lens)
    shape = (lanes_s, heads * samples)
    lane = lax.broadcasted_iota(jnp.int32, shape, 1)
    row = lax.broadcasted_iota(jnp.int32, shape, 0)
    wanted = ids + lax.rem(row, heads) * samples
    pick = jnp.where(lane == wanted, 1.0, 0.0).astype(BF16)

    early[0].wait()
    queries = jnp.concatenate(
        [q_ref[:, g * HD : (g + 1) * HD] for g in range(heads)], axis=0
    )
    early[1].wait()
    early[2].wait()
    keys = prefix_ref[0]
    values_t = prefix_ref[1].T
    pieces = []
    for g in range(heads):
        s = dot_nt(keys, queries[g * samples : (g + 1) * samples])
        high = jnp.max(s, axis=0, keepdims=True) * scale2
        weights = jnp.exp2(s * scale2 - high)
        total = jnp.sum(weights, axis=0, keepdims=True)
        pieces.append((high, total, dot(values_t, weights.astype(BF16))))

    for copy in late:
        copy.wait()
    row_queries = dot(pick, queries)
    per_tile = min(rows, max(1, 128 // heads))
    width = per_tile * heads
    outs, lses = [], []
    for tile in range(rows // per_tile):
        at = tile * per_tile
        q_tile = row_queries[at * heads : at * heads + width]
        own = lax.broadcasted_iota(jnp.int32, (width, HD), 0) // heads
        q_wide = jnp.concatenate(
            [jnp.where(own == r, q_tile, 0.0).astype(BF16) for r in range(per_tile)], axis=1
        )
        row_keys = jnp.concatenate(
            [suffix_ref[0, at + r] for r in range(per_tile)], axis=1
        )
        s = dot_nt(row_keys, q_wide) * scale2
        t = lax.broadcasted_iota(jnp.int32, s.shape, 0)
        s = jnp.where(t < lens[:, at * heads : at * heads + width], s, -jnp.inf)
        high = jnp.max(s, axis=0, keepdims=True)
        weights = jnp.exp2(s - high)
        total = jnp.sum(weights, axis=0, keepdims=True)
        turned = weights.T
        own_t = lax.broadcasted_iota(jnp.int32, (width, span), 0) // heads
        w_wide = jnp.concatenate(
            [jnp.where(own_t == r, turned, 0.0).astype(BF16) for r in range(per_tile)], axis=1
        )
        values = suffix_ref[1, at : at + per_tile].reshape(per_tile * span, HD)
        outs.append(dot(w_wide, values).T / total)
        lses.append(high + jnp.log2(total))
    hi, mid, low = split3(jnp.concatenate(lses, axis=1))
    sub = lax.broadcasted_iota(jnp.int32, (16, lanes_s), 0)
    stats = jnp.where(sub == 0, hi, jnp.where(sub == 1, mid, jnp.where(sub == 2, low, 1.0)))
    to_place = jnp.concatenate([jnp.concatenate(outs, axis=1), stats], axis=0).astype(BF16)
    placed = dot(to_place, pick)
    placed_lse = placed[HD : HD + 1] + placed[HD + 1 : HD + 2] + placed[HD + 2 : HD + 3]
    present = placed[HD + 3 : HD + 4]

    rows_out = []
    for g, (high, total, out) in enumerate(pieces):
        at = slice(g * samples, (g + 1) * samples)
        here = present[:, at] > 0.5
        other = jnp.where(here, placed_lse[:, at], high)
        top = jnp.maximum(high, other)
        own_weight = jnp.exp2(high - top)
        other_weight = jnp.where(here, jnp.exp2(other - top), 0.0)
        both = own_weight * total + other_weight
        out = out * (own_weight / both) + placed[:HD, at] * (other_weight / both)
        msg_ref[g * HD : (g + 1) * HD, :] = out.astype(BF16)
        rows_out.append(top + jnp.log2(both))
    sub = lax.broadcasted_iota(jnp.int32, (STAT_ROWS, samples), 0)
    stats = jnp.zeros((STAT_ROWS, samples), F32)
    for g in range(heads):
        for part, value in enumerate(split3(rows_out[g])):
            stats = jnp.where(sub == part * heads + g, value, stats)
    msg_ref[heads * HD :, :] = stats.astype(BF16)


def attention_piece(where, cache_sample, suffix_length, queries, prefix, suffix, heads):
    samples = queries.shape[0]
    block, rows, span = prefix.shape[1], suffix.shape[1], suffix.shape[2]
    groups = 4 if rows % 4 == 0 else 1
    return run(
        "attention",
        functools.partial(attention_kernel, heads, groups),
        [SCALARS] + [IN_PLACE] * 5,
        [where, cache_sample, suffix_length, queries, prefix, suffix],
        out_specs=WHOLE,
        out_shape=jax.ShapeDtypeStruct((heads * HD + STAT_ROWS, samples), BF16),
        scratch_shapes=[
            pltpu.SMEM(cache_sample.shape, jnp.int32),
            pltpu.SMEM(suffix_length.shape, jnp.int32),
            pltpu.VMEM((samples, heads * HD), BF16),
            pltpu.VMEM((2, block, HD), BF16),
            pltpu.VMEM((2, rows, span, HD), BF16),
            pltpu.SemaphoreType.DMA((2,)),
            pltpu.SemaphoreType.DMA((3 + 2 * groups,)),
        ],
        cost_estimate=cost(5),
        limit=60 * 1024 * 1024,
    )


def merge_kernel(heads, *refs):
    pieces, out_ref = refs[:-1], refs[-1]
    top_rows = heads * HD
    lses = []
    for ref in pieces:
        stats = ref[top_rows:, :].astype(F32)
        lses.append(
            stats[:heads] + stats[heads : 2 * heads] + stats[2 * heads : 3 * heads]
        )
    top = functools.reduce(jnp.maximum, lses)
    weights = [jnp.exp2(lse - top) for lse in lses]
    denom = functools.reduce(jnp.add, weights)
    weights = [w / denom for w in weights]
    for g in range(heads):
        total = None
        for ref, w in zip(pieces, weights):
            term = ref[g * HD : (g + 1) * HD, :].astype(F32) * w[g : g + 1]
            total = term if total is None else total + term
        out_ref[:, g * HD : (g + 1) * HD] = total.T.astype(BF16)


def merge(pieces, heads):
    samples = pieces[0].shape[1]
    return run(
        "merge",
        functools.partial(merge_kernel, heads),
        [WHOLE] * len(pieces),
        pieces,
        out_specs=WHOLE,
        out_shape=jax.ShapeDtypeStruct((samples, heads * HD), BF16),
        cost_estimate=cost(1.3),
    )


def proj_kernel(n_ctx, n_head, own_rows, n_smp, parts, chunks, where_ref, *refs):
    attn_refs, w_hbm, refs = refs[:n_smp], refs[n_smp], refs[n_smp + 1 :]
    out_refs, (full, lhs, w_buf, sems) = refs[:-4], refs[-4:]
    ctx, smp, head = where_ref[0], where_ref[1], where_ref[2]
    samples = attn_refs[0].shape[0]
    tile = w_buf.shape[2]
    copies = [
        pltpu.make_async_copy(
            w_hbm.at[0, :, pl.ds(i * tile, tile)], w_buf.at[i], sems.at[i]
        )
        for i in range(chunks)
    ]
    for copy in copies:
        copy.start()
    for k, ref in enumerate(attn_refs):
        at = lax.rem(smp + n_smp - k, n_smp) * samples
        full[pl.ds(pl.multiple_of(at, 16), samples), :] = ref[...]
    step = own_rows // parts
    to = 0
    for b in range(n_head):
        h = lax.rem(head + b, n_head)
        for p in range(parts):
            for t in range(n_ctx):
                c = lax.rem(ctx + n_ctx - t, n_ctx)
                at = (c * n_head + h) * own_rows + p * step
                lhs[to : to + step, :] = full[pl.ds(pl.multiple_of(at, step), step), :]
                to += step
    for i, copy in enumerate(copies):
        copy.wait()
        out = dot(lhs[...], w_buf[i]).astype(BF16)
        row = 0
        for ref in out_refs:
            ref[:, i * tile : (i + 1) * tile] = out[row : row + ref.shape[0]]
            row += ref.shape[0]


def project(where, attn, w_out, n_ctx, n_head, own_rows, parts):
    n_smp = len(attn)
    samples, depth = attn[0].shape
    width = w_out.shape[2]
    chunks = 4
    tile = width // chunks
    per = n_ctx * own_rows // parts
    rows = per * parts * n_head
    return run(
        "project",
        functools.partial(proj_kernel, n_ctx, n_head, own_rows, n_smp, parts, chunks),
        [SCALARS] + [WHOLE] * n_smp + [IN_PLACE],
        [where, *attn, w_out],
        out_specs=[WHOLE] * (parts + n_head - 1),
        out_shape=[jax.ShapeDtypeStruct((per, width), BF16)] * parts
        + [jax.ShapeDtypeStruct((per * parts, width), BF16)] * (n_head - 1),
        scratch_shapes=[
            pltpu.VMEM((n_smp * samples, depth), BF16),
            pltpu.VMEM((rows, depth), BF16),
            pltpu.VMEM((chunks, depth, tile), BF16),
            pltpu.SemaphoreType.DMA((chunks,)),
        ],
        cost_estimate=cost(5),
    )


def add_heads_kernel(n_ctx, row, keep_ref, *refs):
    recv, outs = refs[:-n_ctx], refs[-n_ctx:]
    rows, width = outs[0].shape[0], recv[0].shape[1]
    pieces = outs[0].shape[1] // width
    for t, ref in enumerate(outs):
        for j in range(pieces):
            columns = slice(j * width, (j + 1) * width)
            total = keep_ref[t * rows : (t + 1) * rows, columns].astype(F32)
            for other in recv[j::pieces]:
                at = row + t * rows
                total = total + other[at : at + rows].astype(F32)
            ref[:, columns] = total.astype(BF16)


def send_heads(sends, pieces):
    step = sends[0].shape[1] // pieces
    return [
        shift(send[:, j * step : (j + 1) * step], "head", len(sends) + 1, b)
        for b, send in enumerate(sends, 1)
        for j in range(pieces)
    ]


def add_heads(keep, recv, row, n_ctx, after=()):
    rows, width = keep.shape
    return run(
        "add_heads",
        functools.partial(add_heads_kernel, n_ctx, row),
        [WHOLE] * (1 + len(recv)),
        [keep, *recv],
        after,
        out_specs=[WHOLE] * n_ctx,
        out_shape=[jax.ShapeDtypeStruct((rows // n_ctx, width), BF16)] * n_ctx,
    )


def far_first(n):
    return sorted(range(1, n), key=lambda k: -min(k, n - k))


def send_sums(sums):
    n_ctx = len(sums)
    return [sums[0]] + [shift(sums[t], "ctx", n_ctx, -t) for t in far_first(n_ctx)]


def send_rows(x, n_ctx):
    got = {t: shift(x, "ctx", n_ctx, t) for t in far_first(n_ctx)}
    return [x] + [got[t] for t in range(1, n_ctx)]


def join_kernel(*refs):
    pieces, out_ref = refs[:-1], refs[-1]
    rows = pieces[0].shape[0]
    for t, ref in enumerate(pieces):
        out_ref[t * rows : (t + 1) * rows, :] = ref[...]


def join(pieces, after):
    rows, width = pieces[0].shape
    return run(
        "join",
        join_kernel,
        [WHOLE] * len(pieces),
        pieces,
        after,
        out_specs=WHOLE,
        out_shape=jax.ShapeDtypeStruct((rows * len(pieces), width), BF16),
    )


def state_kernel(n_pieces, *refs):
    pieces, (res_ref, gain_ref, state_ref, msg_ref) = refs[:n_pieces], refs[n_pieces:]
    width = res_ref.shape[1]
    total = res_ref[...].astype(F32)
    for ref in pieces:
        total = total + ref[...].astype(F32)
    state = total.astype(BF16)
    state_ref[...] = state
    wide = state.astype(F32)
    msg_ref[:, :width] = (wide * gain_ref[...]).astype(BF16)
    hi, mid, low = split3(jnp.sum(wide * wide, axis=1, keepdims=True))
    lane = lax.broadcasted_iota(jnp.int32, (hi.shape[0], HD), 1)
    stats = jnp.where(
        lane == 0, hi, jnp.where(lane == 1, mid, jnp.where(lane == 2, low, 0.0))
    )
    msg_ref[:, width:] = stats.astype(BF16)


def make_state(pieces, residual, gain, after):
    rows, width = residual.shape
    return run(
        "state",
        functools.partial(state_kernel, len(pieces)),
        [WHOLE] * (len(pieces) + 2),
        [*pieces, residual, gain],
        after,
        out_specs=[WHOLE] * 2,
        out_shape=[
            jax.ShapeDtypeStruct((rows, width), BF16),
            jax.ShapeDtypeStruct((rows, width + HD), BF16),
        ],
    )


def finish_kernel(*refs):
    total = refs[0][...].astype(F32)
    for ref in refs[1:-1]:
        total = total + ref[...].astype(F32)
    refs[-1][...] = total.astype(refs[-1].dtype)


def finish(pieces):
    total = pieces[-1]
    for i in reversed(range(len(pieces) - 1)):
        total = run(
            "finish",
            finish_kernel,
            [WHOLE] * 2,
            [total, pieces[i]],
            out_specs=WHOLE,
            out_shape=jax.ShapeDtypeStruct(total.shape, F32 if i else BF16),
        )
    return total


def gate_up_kernel(chunks, n_parts, where_ref, *refs):
    parts, (g_hbm, u_hbm, out_ref, x, acc, g_buf, u_buf, g_sem, u_sem) = (
        refs[:n_parts],
        refs[n_parts:],
    )
    tile, units = g_buf.shape[1:]
    at = pl.multiple_of(where_ref[0] * units, 128)

    def chunk_copy(i, which):
        hbm, buf, sem = ((g_hbm, g_buf, g_sem), (u_hbm, u_buf, u_sem))[which]
        from_at = pl.multiple_of(i * tile, tile)
        return pltpu.make_async_copy(
            hbm.at[pl.ds(from_at, tile), pl.ds(at, units)], buf.at[i], sem.at[i]
        )

    for i in range(chunks):
        chunk_copy(i, 0).start()
        chunk_copy(i, 1).start()
    row = 0
    for ref in parts:
        x[row : row + ref.shape[0]] = ref[:, : x.shape[1]]
        row += ref.shape[0]
    acc[...] = jnp.zeros_like(acc)
    turns = 2

    @pl.loop(0, turns)
    def _(turn):
        gate = up = None
        for j in range(chunks // turns):
            i = turn * (chunks // turns) + j
            lhs = x[:, pl.ds(pl.multiple_of(i * tile, tile), tile)]
            chunk_copy(i, 0).wait()
            term = dot(lhs, g_buf[i])
            gate = term if gate is None else gate + term
            chunk_copy(i, 1).wait()
            term = dot(lhs, u_buf[i])
            up = term if up is None else up + term
        acc[:, :units] += gate
        acc[:, units:] += up

    out_ref[:, : 2 * units] = acc[...].astype(out_ref.dtype)
    row = 0
    for ref in parts:
        out_ref[row : row + ref.shape[0], 2 * units :] = ref[:, x.shape[1] :].astype(
            out_ref.dtype
        )
        row += ref.shape[0]


def gate_up(block, parts, gate_matrix, w_up, units, dtype, after=()):
    rows, depth = sum(p.shape[0] for p in parts), gate_matrix.shape[0]
    chunks = 8
    tile = depth // chunks
    return run(
        "gate_up",
        functools.partial(gate_up_kernel, chunks, len(parts)),
        [SCALARS] + [WHOLE] * len(parts) + [IN_PLACE] * 2,
        [block.reshape(1), *parts, gate_matrix, w_up],
        after,
        out_specs=WHOLE,
        out_shape=jax.ShapeDtypeStruct((rows, 2 * units + HD), dtype),
        scratch_shapes=[pltpu.VMEM((rows, depth), BF16), pltpu.VMEM((rows, 2 * units), F32)]
        + [pltpu.VMEM((chunks, tile, units), BF16)] * 2
        + [pltpu.SemaphoreType.DMA((chunks,))] * 2,
        cost_estimate=cost(2 + 4.2 * units / 1024),
    )


def act_kernel(own_ref, *refs):
    recv, out_ref = refs[:-1], refs[-1]
    total = own_ref[...]
    for ref in recv:
        total = total + ref[...].astype(F32)
    units = out_ref.shape[1]
    square = jnp.sum(total[:, 2 * units :], axis=1, keepdims=True)
    factor = lax.rsqrt(square / D + EPSILON)
    gate = factor * total[:, :units]
    up = factor * total[:, units : 2 * units]
    out_ref[...] = (gate / (1.0 + jnp.exp(-gate)) * up).astype(BF16)


def activate(own, recv, units, after):
    return run(
        "activate",
        act_kernel,
        [WHOLE] * (1 + len(recv)),
        [own, *recv],
        after,
        out_specs=WHOLE,
        out_shape=jax.ShapeDtypeStruct((own.shape[0], units), BF16),
    )


def down_kernel(n_parts, chunks, has_acc, last, n_head, where_ref, *refs):
    xs, refs = refs[:n_parts], refs[n_parts:]
    if has_acc:
        acc_ref, w_hbm, *outs, w_buf, sems = refs
    else:
        w_hbm, *outs, w_buf, sems = refs
    units, tile = w_buf.shape[2:]
    copies = []
    for i in range(chunks):
        for p in range(n_parts):
            at = pl.multiple_of(where_ref[p] * units, 16)
            copies.append(
                pltpu.make_async_copy(
                    w_hbm.at[pl.ds(at, units), pl.ds(i * tile, tile)],
                    w_buf.at[i, p],
                    sems.at[i, p],
                )
            )
    for copy in copies:
        copy.start()
    for i in range(chunks):
        total = acc_ref[:, i * tile : (i + 1) * tile] if has_acc else None
        for p in range(n_parts):
            copies[i * n_parts + p].wait()
            term = dot(xs[p][...], w_buf[i, p])
            total = term if total is None else total + term
        if last:
            per = total.shape[0] // n_head
            for b in range(n_head):
                outs[b][:, i * tile : (i + 1) * tile] = total[
                    b * per : (b + 1) * per
                ].astype(BF16)
        else:
            outs[0][:, i * tile : (i + 1) * tile] = total


def down(blocks, xs, w_down, acc, last, n_head, after):
    rows, units = xs[0].shape
    width = w_down.shape[1]
    chunks = 4
    tile = width // chunks
    n = len(xs)
    args = list(xs) + ([] if acc is None else [acc])
    if last:
        out_shape = [jax.ShapeDtypeStruct((rows // n_head, width), BF16)] * n_head
    else:
        out_shape = [jax.ShapeDtypeStruct((rows, width), F32)]
    out = run(
        "down",
        functools.partial(down_kernel, n, chunks, acc is not None, last, n_head),
        [SCALARS] + [WHOLE] * len(args) + [IN_PLACE],
        [jnp.stack(blocks), *args, w_down],
        after,
        out_specs=[WHOLE] * len(out_shape),
        out_shape=out_shape,
        scratch_shapes=[
            pltpu.VMEM((chunks, n, units, tile), BF16),
            pltpu.SemaphoreType.DMA((chunks, n)),
        ],
        cost_estimate=cost(4 * n),
    )
    return out if last else out[0]


def on_device(
    n_ctx,
    n_smp,
    n_head,
    queries,
    prefix_cache,
    suffix_cache,
    suffix_length,
    cache_sample,
    residual,
    w_out,
    norm_gain,
    gate_matrix,
    w_up,
    w_down,
):
    ctx, smp, head = (lax.axis_index(name) for name in ("ctx", "smp", "head"))
    samples = queries.shape[0]
    own_rows = residual.shape[0]
    queries = queries.reshape(samples, -1)
    prefix = prefix_cache.reshape(2, prefix_cache.shape[1], -1)
    rows, span = suffix_cache.shape[1:3]
    suffix = suffix_cache.reshape(2, rows, span, -1)
    kv_heads = prefix.shape[2] // HD
    group = QUERY_HEADS // KEY_VALUE_HEADS
    heads = kv_heads * group // n_ctx

    base = (ctx * n_smp + smp) * rows
    pieces = []
    for k in far_first(n_ctx) + [0]:
        chunk = (ctx + k) % n_ctx
        kv = chunk * heads // group
        at = jnp.stack([chunk, kv, base])
        piece = attention_piece(
            at, cache_sample, suffix_length, queries, prefix, suffix, heads
        )
        pieces.append(shift(piece, "ctx", n_ctx, k) if k else piece)

    parts = 2 if own_rows % 32 == 0 else 1
    step = own_rows // parts
    where = jnp.stack([ctx, smp, head])
    every = range(parts)
    others = range(1, n_smp)
    attn = merge(pieces, heads)
    gathered = [attn] + [shift(attn, "smp", n_smp, k) for k in others]
    by_head = project(where, gathered, w_out, n_ctx, n_head, own_rows, parts)
    recv = send_heads(by_head[parts:], 1)
    all_sums = [
        add_heads(by_head[p], recv, p * by_head[p].shape[0], n_ctx) for p in every
    ]
    units = gate_matrix.shape[1] // n_smp
    states, rows, full = [None] * parts, [None] * parts, [None] * parts
    received, own, hidden, theirs = ([None] * parts for _ in range(4))
    sums = [None] * parts
    done = []

    def state_step(p):
        nonlocal done
        states[p], message = make_state(
            send_sums(all_sums[p]), residual[p * step : (p + 1) * step], gain, done
        )
        rows[p] = send_rows(message, n_ctx)
        done = [states[p]]

    def others_step(p):
        nonlocal done
        joined = join(rows[p], done)
        full[p] = [shift(joined, "head", n_head, b) if b else joined for b in range(n_head)]
        received[p] = []
        for k in others:
            block = (smp + k) % n_smp
            send = gate_up(block, full[p], gate_matrix, w_up, units, BF16, done)
            done = [send]
            received[p].append(shift(send, "smp", n_smp, k))

    def own_step(p):
        nonlocal done
        own[p] = gate_up(smp, full[p], gate_matrix, w_up, units, F32, done)
        done = [own[p]]

    def hidden_step(p):
        nonlocal done
        hidden[p] = activate(own[p], received[p], units, done)
        theirs[p] = [shift(hidden[p], "smp", n_smp, k) for k in others]
        done = [hidden[p]]

    blocks = [(smp + n_smp - k) % n_smp for k in range(n_smp)]

    def down_step(p, first, count, acc):
        nonlocal done
        xs = [hidden[p], *theirs[p]][first : first + count]
        last = first + count == n_smp
        out = down(blocks[first : first + count], xs, w_down, acc, last, n_head, done)
        done = [out[0] if last else out]
        return out

    gain = norm_gain[None, :]
    state_step(0)
    for p in every:
        others_step(p)
        if p + 1 < parts:
            state_step(p + 1)
            own_step(p)
            hidden_step(p)
            continue
        own_step(p)
        for q in range(p):
            keep, *sends = down_step(q, 0, n_smp, None)
            sums[q] = add_heads(keep, send_heads(sends, 1), 0, n_ctx)
        hidden_step(p)
        acc = down_step(p, 0, 1, None)
        outs = [finish([states[q], *send_sums(sums[q])]) for q in range(p)]
        done = done + outs
        keep, *sends = down_step(p, 1, n_smp - 1, acc)
    sums[-1] = add_heads(keep, send_heads(sends, PIECES), 0, n_ctx)
    outs.append(finish([states[-1], *send_sums(sums[-1])]))
    return jnp.concatenate(outs, axis=0)


def solution(mesh):
    in_specs = (
        P(("group", "smp"), "head", None),
        P(None, ("group", "ctx"), "head", None),
        P(None, ("group", "ctx", "smp"), None, "head", None),
        P(("group", "smp")),
        P("group"),
        P(("group", "ctx", "head"), "smp"),
        P("head", "ctx", "smp"),
        P("smp"),
        P("smp", ("ctx", "head")),
        P("smp", ("ctx", "head")),
        P(("ctx", "head"), "smp"),
    )
    out_specs = P(("group", "ctx", "head"), "smp")
    body = functools.partial(
        on_device, mesh.shape["ctx"], mesh.shape["smp"], mesh.shape["head"]
    )
    return jax.shard_map(
        body, mesh=mesh, in_specs=in_specs, out_specs=out_specs, check_vma=False
    )
```

```python
import functools

import jax
import jax.numpy as jnp
from jax import lax
from jax.experimental import pallas as pl
from jax.experimental.pallas import tpu as pltpu
from jax.sharding import PartitionSpec as P

D = 8192
QUERY_HEADS = 64
KEY_VALUE_HEADS = 8
HD = 128
EPSILON = 1e-05

BF16 = jnp.bfloat16
F32 = jnp.float32
VMEM_LIMIT = 48 * 1024 * 1024
STAT_ROWS = 32
PIECES = 4
LOG2E = 1.4426950408889634
LN2 = 0.6931471805599453


def params(limit=VMEM_LIMIT):
    return pltpu.CompilerParams(vmem_limit_bytes=limit)


def cost(us):
    return pl.CostEstimate(
        flops=int(us * 1.1e9), bytes_accessed=int(us * 3.6e6), transcendentals=0
    )


IN_PLACE = pl.BlockSpec(memory_space=pl.ANY)
WHOLE = pl.BlockSpec(memory_space=pltpu.VMEM)
SCALARS = pl.BlockSpec(memory_space=pltpu.SMEM)


def run(name, kernel, in_specs, args, after=(), limit=VMEM_LIMIT, **more):
    n, m = len(args), len(after)

    def body(*refs):
        return kernel(*refs[:n], *refs[n + m :])

    return pl.pallas_call(
        body,
        name=name,
        in_specs=list(in_specs) + [IN_PLACE] * m,
        compiler_params=params(limit),
        **{"cost_estimate": cost(0.2), **more},
    )(*args, *after)


def dot(a, b):
    return jnp.dot(a, b, preferred_element_type=F32)


def dot_nt(a, b):
    return lax.dot_general(a, b, (((1,), (1,)), ((), ())), preferred_element_type=F32)


def split3(x):
    hi = x.astype(BF16).astype(F32)
    mid = (x - hi).astype(BF16).astype(F32)
    low = (x - hi - mid).astype(BF16).astype(F32)
    return hi, mid, low


def shift(x, axis, size, k):
    return lax.ppermute(x, axis, [(i, (i + k) % size) for i in range(size)])


def attention_kernel(
    heads,
    group,
    ahead,
    groups,
    where_ref,
    sample_hbm,
    length_hbm,
    q_hbm,
    prefix_hbm,
    suffix_hbm,
    msg_ref,
    sample_ref,
    length_ref,
    q_ref,
    prefix_ref,
    suffix_ref,
    number_sems,
    sems,
):
    samples = q_ref.shape[0]
    rows, span = suffix_ref.shape[1:3]
    lanes_s = rows * heads
    scale2 = HD**-0.5 * LOG2E
    n_ctx = q_hbm.shape[1] // (heads * HD)
    chunk = lax.rem(where_ref[0] + ahead, n_ctx)
    kv = lax.div(chunk * heads, group)
    q_at = pl.ds(pl.multiple_of(chunk * (heads * HD), HD), heads * HD)
    kv_at = pl.ds(pl.multiple_of(kv * HD, HD), HD)
    numbers = [
        pltpu.make_async_copy(sample_hbm, sample_ref, number_sems.at[0]),
        pltpu.make_async_copy(length_hbm, length_ref, number_sems.at[1]),
    ]
    early = [
        pltpu.make_async_copy(q_hbm.at[:, q_at], q_ref, sems.at[0]),
        pltpu.make_async_copy(prefix_hbm.at[0, :, kv_at], prefix_ref.at[0], sems.at[1]),
        pltpu.make_async_copy(prefix_hbm.at[1, :, kv_at], prefix_ref.at[1], sems.at[2]),
    ]
    late = []
    some = rows // groups
    for which in range(2):
        for g in range(groups):
            part = pl.ds(g * some, some)
            late.append(
                pltpu.make_async_copy(
                    suffix_hbm.at[which, part, :, kv_at],
                    suffix_ref.at[which, part],
                    sems.at[3 + which * groups + g],
                )
            )
    for copy in numbers + early + late:
        copy.start()

    for copy in numbers:
        copy.wait()
    column = lax.broadcasted_iota(jnp.int32, (lanes_s, 1), 0) // heads
    across = lax.broadcasted_iota(jnp.int32, (1, lanes_s), 1) // heads
    ids = jnp.zeros((lanes_s, 1), jnp.int32)
    lens = jnp.zeros((1, lanes_s), jnp.int32)
    for r in range(rows):
        sample = lax.rem(sample_ref[where_ref[3] + r], samples)
        ids = jnp.where(column == r, sample, ids)
        lens = jnp.where(across == r, length_ref[sample], lens)
    shape = (lanes_s, heads * samples)
    lane = lax.broadcasted_iota(jnp.int32, shape, 1)
    row = lax.broadcasted_iota(jnp.int32, shape, 0)
    wanted = ids + lax.rem(row, heads) * samples
    pick = jnp.where(lane == wanted, 1.0, 0.0).astype(BF16)

    early[0].wait()
    queries = jnp.concatenate(
        [q_ref[:, g * HD : (g + 1) * HD] for g in range(heads)], axis=0
    )
    early[1].wait()
    early[2].wait()
    keys = prefix_ref[0]
    values_t = prefix_ref[1].T
    pieces = []
    for g in range(heads):
        s = dot_nt(keys, queries[g * samples : (g + 1) * samples])
        high = jnp.max(s, axis=0, keepdims=True) * scale2
        weights = jnp.exp2(s * scale2 - high)
        total = jnp.sum(weights, axis=0, keepdims=True)
        pieces.append((high, total, dot(values_t, weights.astype(BF16))))

    for copy in late:
        copy.wait()
    row_queries = dot(pick, queries)
    per_tile = min(rows, max(1, 128 // heads))
    width = per_tile * heads
    outs, lses = [], []
    for tile in range(rows // per_tile):
        at = tile * per_tile
        q_tile = row_queries[at * heads : at * heads + width]
        own = lax.broadcasted_iota(jnp.int32, (width, HD), 0) // heads
        q_wide = jnp.concatenate(
            [jnp.where(own == r, q_tile, 0.0).astype(BF16) for r in range(per_tile)], axis=1
        )
        row_keys = jnp.concatenate(
            [suffix_ref[0, at + r] for r in range(per_tile)], axis=1
        )
        s = dot_nt(row_keys, q_wide) * scale2
        t = lax.broadcasted_iota(jnp.int32, s.shape, 0)
        s = jnp.where(t < lens[:, at * heads : at * heads + width], s, -jnp.inf)
        high = jnp.max(s, axis=0, keepdims=True)
        weights = jnp.exp2(s - high)
        total = jnp.sum(weights, axis=0, keepdims=True)
        turned = weights.T
        own_t = lax.broadcasted_iota(jnp.int32, (width, span), 0) // heads
        w_wide = jnp.concatenate(
            [jnp.where(own_t == r, turned, 0.0).astype(BF16) for r in range(per_tile)], axis=1
        )
        values = suffix_ref[1, at : at + per_tile].reshape(per_tile * span, HD)
        outs.append(dot(w_wide, values).T / total)
        lses.append(high + jnp.log2(total))
    hi, mid, low = split3(jnp.concatenate(lses, axis=1))
    sub = lax.broadcasted_iota(jnp.int32, (16, lanes_s), 0)
    stats = jnp.where(sub == 0, hi, jnp.where(sub == 1, mid, jnp.where(sub == 2, low, 1.0)))
    to_place = jnp.concatenate([jnp.concatenate(outs, axis=1), stats], axis=0).astype(BF16)
    placed = dot(to_place, pick)
    placed_lse = placed[HD : HD + 1] + placed[HD + 1 : HD + 2] + placed[HD + 2 : HD + 3]
    present = placed[HD + 3 : HD + 4]

    rows_out = []
    for g, (high, total, out) in enumerate(pieces):
        at = slice(g * samples, (g + 1) * samples)
        here = present[:, at] > 0.5
        other = jnp.where(here, placed_lse[:, at], high)
        top = jnp.maximum(high, other)
        own_weight = jnp.exp2(high - top)
        other_weight = jnp.where(here, jnp.exp2(other - top), 0.0)
        both = own_weight * total + other_weight
        out = out * (own_weight / both) + placed[:HD, at] * (other_weight / both)
        msg_ref[g * HD : (g + 1) * HD, :] = out.astype(BF16)
        rows_out.append(top + jnp.log2(both))
    sub = lax.broadcasted_iota(jnp.int32, (STAT_ROWS, samples), 0)
    stats = jnp.zeros((STAT_ROWS, samples), F32)
    for g in range(heads):
        for part, value in enumerate(split3(rows_out[g])):
            stats = jnp.where(sub == part * heads + g, value, stats)
    msg_ref[heads * HD :, :] = stats.astype(BF16)


def attention_piece(
    ahead, where, cache_sample, suffix_length, queries, prefix, suffix, heads, group
):
    samples = queries.shape[0]
    block, rows, span = prefix.shape[1], suffix.shape[1], suffix.shape[2]
    groups = 4 if rows % 4 == 0 else 1
    return run(
        "attention",
        functools.partial(attention_kernel, heads, group, ahead, groups),
        [SCALARS] + [IN_PLACE] * 5,
        [where, cache_sample, suffix_length, queries, prefix, suffix],
        out_specs=WHOLE,
        out_shape=jax.ShapeDtypeStruct((heads * HD + STAT_ROWS, samples), BF16),
        scratch_shapes=[
            pltpu.SMEM(cache_sample.shape, jnp.int32),
            pltpu.SMEM(suffix_length.shape, jnp.int32),
            pltpu.VMEM((samples, heads * HD), BF16),
            pltpu.VMEM((2, block, HD), BF16),
            pltpu.VMEM((2, rows, span, HD), BF16),
            pltpu.SemaphoreType.DMA((2,)),
            pltpu.SemaphoreType.DMA((3 + 2 * groups,)),
        ],
        cost_estimate=cost(5),
        limit=60 * 1024 * 1024,
    )


def merge_kernel(heads, *refs):
    pieces, out_ref = refs[:-1], refs[-1]
    top_rows = heads * HD
    lses = []
    for ref in pieces:
        stats = ref[top_rows:, :].astype(F32)
        lses.append(
            stats[:heads] + stats[heads : 2 * heads] + stats[2 * heads : 3 * heads]
        )
    top = functools.reduce(jnp.maximum, lses)
    weights = [jnp.exp2(lse - top) for lse in lses]
    denom = functools.reduce(jnp.add, weights)
    weights = [w / denom for w in weights]
    for g in range(heads):
        total = None
        for ref, w in zip(pieces, weights):
            term = ref[g * HD : (g + 1) * HD, :].astype(F32) * w[g : g + 1]
            total = term if total is None else total + term
        out_ref[:, g * HD : (g + 1) * HD] = total.T.astype(BF16)


def merge(pieces, heads):
    samples = pieces[0].shape[1]
    return run(
        "merge",
        functools.partial(merge_kernel, heads),
        [WHOLE] * len(pieces),
        pieces,
        out_specs=WHOLE,
        out_shape=jax.ShapeDtypeStruct((samples, heads * HD), BF16),
        cost_estimate=cost(1.3),
    )


def proj_kernel(n_ctx, n_head, own_rows, n_smp, parts, chunks, where_ref, *refs):
    attn_refs, w_hbm, refs = refs[:n_smp], refs[n_smp], refs[n_smp + 1 :]
    out_refs, (full, lhs, w_buf, sems) = refs[:-4], refs[-4:]
    ctx, smp, head = where_ref[0], where_ref[1], where_ref[2]
    samples = attn_refs[0].shape[0]
    tile = w_buf.shape[2]
    copies = [
        pltpu.make_async_copy(
            w_hbm.at[0, :, pl.ds(i * tile, tile)], w_buf.at[i], sems.at[i]
        )
        for i in range(chunks)
    ]
    for copy in copies:
        copy.start()
    for k, ref in enumerate(attn_refs):
        at = lax.rem(smp + n_smp - k, n_smp) * samples
        full[pl.ds(pl.multiple_of(at, 16), samples), :] = ref[...]
    step = own_rows // parts
    to = 0
    for b in range(n_head):
        h = lax.rem(head + b, n_head)
        for p in range(parts):
            for t in range(n_ctx):
                c = lax.rem(ctx + n_ctx - t, n_ctx)
                at = (c * n_head + h) * own_rows + p * step
                lhs[to : to + step, :] = full[pl.ds(pl.multiple_of(at, step), step), :]
                to += step
    for i, copy in enumerate(copies):
        copy.wait()
        out = dot(lhs[...], w_buf[i]).astype(BF16)
        row = 0
        for ref in out_refs:
            ref[:, i * tile : (i + 1) * tile] = out[row : row + ref.shape[0]]
            row += ref.shape[0]


def project(where, attn, w_out, n_ctx, n_head, own_rows, parts):
    n_smp = len(attn)
    samples, depth = attn[0].shape
    width = w_out.shape[2]
    chunks = 4
    tile = width // chunks
    per = n_ctx * own_rows // parts
    rows = per * parts * n_head
    return run(
        "project",
        functools.partial(proj_kernel, n_ctx, n_head, own_rows, n_smp, parts, chunks),
        [SCALARS] + [WHOLE] * n_smp + [IN_PLACE],
        [where, *attn, w_out],
        out_specs=[WHOLE] * (parts + n_head - 1),
        out_shape=[jax.ShapeDtypeStruct((per, width), BF16)] * parts
        + [jax.ShapeDtypeStruct((per * parts, width), BF16)] * (n_head - 1),
        scratch_shapes=[
            pltpu.VMEM((n_smp * samples, depth), BF16),
            pltpu.VMEM((rows, depth), BF16),
            pltpu.VMEM((chunks, depth, tile), BF16),
            pltpu.SemaphoreType.DMA((chunks,)),
        ],
        cost_estimate=cost(5),
    )


def add_heads_kernel(n_ctx, row, keep_ref, *refs):
    recv, outs = refs[:-n_ctx], refs[-n_ctx:]
    rows, width = outs[0].shape[0], recv[0].shape[1]
    pieces = outs[0].shape[1] // width
    for t, ref in enumerate(outs):
        for j in range(pieces):
            columns = slice(j * width, (j + 1) * width)
            total = keep_ref[t * rows : (t + 1) * rows, columns].astype(F32)
            for other in recv[j::pieces]:
                at = row + t * rows
                total = total + other[at : at + rows].astype(F32)
            ref[:, columns] = total.astype(BF16)


def send_heads(sends, pieces):
    step = sends[0].shape[1] // pieces
    return [
        shift(send[:, j * step : (j + 1) * step], "head", len(sends) + 1, b)
        for b, send in enumerate(sends, 1)
        for j in range(pieces)
    ]


def add_heads(keep, recv, row, n_ctx, after=()):
    rows, width = keep.shape
    return run(
        "add_heads",
        functools.partial(add_heads_kernel, n_ctx, row),
        [WHOLE] * (1 + len(recv)),
        [keep, *recv],
        after,
        out_specs=[WHOLE] * n_ctx,
        out_shape=[jax.ShapeDtypeStruct((rows // n_ctx, width), BF16)] * n_ctx,
    )


def far_first(n):
    return sorted(range(1, n), key=lambda k: -min(k, n - k))


def send_sums(sums):
    n_ctx = len(sums)
    return [sums[0]] + [shift(sums[t], "ctx", n_ctx, -t) for t in far_first(n_ctx)]


def send_rows(x, n_ctx):
    got = {t: shift(x, "ctx", n_ctx, t) for t in far_first(n_ctx)}
    return [x] + [got[t] for t in range(1, n_ctx)]


def join_kernel(*refs):
    pieces, out_ref = refs[:-1], refs[-1]
    rows = pieces[0].shape[0]
    for t, ref in enumerate(pieces):
        out_ref[t * rows : (t + 1) * rows, :] = ref[...]


def join(pieces, after):
    rows, width = pieces[0].shape
    return run(
        "join",
        join_kernel,
        [WHOLE] * len(pieces),
        pieces,
        after,
        out_specs=WHOLE,
        out_shape=jax.ShapeDtypeStruct((rows * len(pieces), width), BF16),
    )


def state_kernel(n_pieces, *refs):
    pieces, (res_ref, gain_ref, state_ref, msg_ref) = refs[:n_pieces], refs[n_pieces:]
    width = res_ref.shape[1]
    total = res_ref[...].astype(F32)
    for ref in pieces:
        total = total + ref[...].astype(F32)
    state = total.astype(BF16)
    state_ref[...] = state
    wide = state.astype(F32)
    msg_ref[:, :width] = (wide * gain_ref[...]).astype(BF16)
    hi, mid, low = split3(jnp.sum(wide * wide, axis=1, keepdims=True))
    lane = lax.broadcasted_iota(jnp.int32, (hi.shape[0], HD), 1)
    stats = jnp.where(
        lane == 0, hi, jnp.where(lane == 1, mid, jnp.where(lane == 2, low, 0.0))
    )
    msg_ref[:, width:] = stats.astype(BF16)


def make_state(pieces, residual, gain, after):
    rows, width = residual.shape
    return run(
        "state",
        functools.partial(state_kernel, len(pieces)),
        [WHOLE] * (len(pieces) + 2),
        [*pieces, residual, gain],
        after,
        out_specs=[WHOLE] * 2,
        out_shape=[
            jax.ShapeDtypeStruct((rows, width), BF16),
            jax.ShapeDtypeStruct((rows, width + HD), BF16),
        ],
        cost_estimate=cost(8),
    )


def finish_kernel(above, *refs):
    terms, out_ref = refs[above:-1], refs[-1]
    total = terms[0][...].astype(F32)
    for ref in terms[1:]:
        total = total + ref[...].astype(F32)
    row = 0
    for ref in refs[:above]:
        out_ref[row : row + ref.shape[0], :] = ref[...]
        row += ref.shape[0]
    out_ref[row:, :] = total.astype(out_ref.dtype)


def finish(pieces, above=()):
    total = pieces[-1]
    for i in reversed(range(len(pieces) - 1)):
        on_top = list(above) if i == 0 else []
        rows, width = total.shape
        shape = (sum(x.shape[0] for x in on_top) + rows, width)
        total = run(
            "finish",
            functools.partial(finish_kernel, len(on_top)),
            [WHOLE] * (len(on_top) + 2),
            [*on_top, total, pieces[i]],
            out_specs=WHOLE,
            out_shape=jax.ShapeDtypeStruct(shape, F32 if i else BF16),
        )
    return total


def gate_up_kernel(chunks, n_parts, where_ref, *refs):
    parts, (g_hbm, u_hbm, out_ref, x, acc, g_buf, u_buf, g_sem, u_sem) = (
        refs[:n_parts],
        refs[n_parts:],
    )
    tile, units = g_buf.shape[1:]
    at = pl.multiple_of(where_ref[0] * units, 128)

    def chunk_copy(i, which):
        hbm, buf, sem = ((g_hbm, g_buf, g_sem), (u_hbm, u_buf, u_sem))[which]
        from_at = pl.multiple_of(i * tile, tile)
        return pltpu.make_async_copy(
            hbm.at[pl.ds(from_at, tile), pl.ds(at, units)], buf.at[i], sem.at[i]
        )

    for i in range(chunks):
        chunk_copy(i, 0).start()
        chunk_copy(i, 1).start()
    row = 0
    for ref in parts:
        x[row : row + ref.shape[0]] = ref[:, : x.shape[1]]
        row += ref.shape[0]
    acc[...] = jnp.zeros_like(acc)
    turns = 2

    @pl.loop(0, turns)
    def _(turn):
        gate = up = None
        for j in range(chunks // turns):
            i = turn * (chunks // turns) + j
            lhs = x[:, pl.ds(pl.multiple_of(i * tile, tile), tile)]
            chunk_copy(i, 0).wait()
            term = dot(lhs, g_buf[i])
            gate = term if gate is None else gate + term
            chunk_copy(i, 1).wait()
            term = dot(lhs, u_buf[i])
            up = term if up is None else up + term
        acc[:, :units] += gate
        acc[:, units:] += up

    out_ref[:, : 2 * units] = acc[...].astype(out_ref.dtype)
    row = 0
    for ref in parts:
        out_ref[row : row + ref.shape[0], 2 * units :] = ref[:, x.shape[1] :].astype(
            out_ref.dtype
        )
        row += ref.shape[0]


def gate_up(block, parts, gate_matrix, w_up, units, dtype, after=()):
    rows, depth = sum(p.shape[0] for p in parts), gate_matrix.shape[0]
    chunks = 8
    tile = depth // chunks
    return run(
        "gate_up",
        functools.partial(gate_up_kernel, chunks, len(parts)),
        [SCALARS] + [WHOLE] * len(parts) + [IN_PLACE] * 2,
        [block.reshape(1), *parts, gate_matrix, w_up],
        after,
        out_specs=WHOLE,
        out_shape=jax.ShapeDtypeStruct((rows, 2 * units + HD), dtype),
        scratch_shapes=[pltpu.VMEM((rows, depth), BF16), pltpu.VMEM((rows, 2 * units), F32)]
        + [pltpu.VMEM((chunks, tile, units), BF16)] * 2
        + [pltpu.SemaphoreType.DMA((chunks,))] * 2,
        cost_estimate=cost(6 if dtype == BF16 else 1),
    )


def act_kernel(own_ref, *refs):
    recv, out_ref = refs[:-1], refs[-1]
    total = own_ref[...]
    for ref in recv:
        total = total + ref[...].astype(F32)
    units = out_ref.shape[1]
    square = jnp.sum(total[:, 2 * units :], axis=1, keepdims=True)
    factor = lax.rsqrt(square / D + EPSILON)
    gate = factor * total[:, :units]
    up = factor * total[:, units : 2 * units]
    out_ref[...] = (gate / (1.0 + jnp.exp(-gate)) * up).astype(BF16)


def activate(own, recv, units, after):
    return run(
        "activate",
        act_kernel,
        [WHOLE] * (1 + len(recv)),
        [own, *recv],
        after,
        out_specs=WHOLE,
        out_shape=jax.ShapeDtypeStruct((own.shape[0], units), BF16),
    )


def down_kernel(n_parts, chunks, has_acc, last, n_head, where_ref, *refs):
    xs, refs = refs[:n_parts], refs[n_parts:]
    if has_acc:
        acc_ref, w_hbm, *outs, w_buf, sems = refs
    else:
        w_hbm, *outs, w_buf, sems = refs
    units, tile = w_buf.shape[2:]
    copies = []
    for i in range(chunks):
        for p in range(n_parts):
            at = pl.multiple_of(where_ref[p] * units, 16)
            copies.append(
                pltpu.make_async_copy(
                    w_hbm.at[pl.ds(at, units), pl.ds(i * tile, tile)],
                    w_buf.at[i, p],
                    sems.at[i, p],
                )
            )
    for copy in copies:
        copy.start()
    for i in range(chunks):
        total = acc_ref[:, i * tile : (i + 1) * tile] if has_acc else None
        for p in range(n_parts):
            copies[i * n_parts + p].wait()
            term = dot(xs[p][...], w_buf[i, p])
            total = term if total is None else total + term
        if last:
            per = total.shape[0] // n_head
            for b in range(n_head):
                outs[b][:, i * tile : (i + 1) * tile] = total[
                    b * per : (b + 1) * per
                ].astype(BF16)
        else:
            outs[0][:, i * tile : (i + 1) * tile] = total


def down(blocks, xs, w_down, acc, last, n_head, after):
    rows, units = xs[0].shape
    width = w_down.shape[1]
    chunks = 4
    tile = width // chunks
    n = len(xs)
    args = list(xs) + ([] if acc is None else [acc])
    if last:
        out_shape = [jax.ShapeDtypeStruct((rows // n_head, width), BF16)] * n_head
    else:
        out_shape = [jax.ShapeDtypeStruct((rows, width), F32)]
    out = run(
        "down",
        functools.partial(down_kernel, n, chunks, acc is not None, last, n_head),
        [SCALARS] + [WHOLE] * len(args) + [IN_PLACE],
        [jnp.stack(blocks), *args, w_down],
        after,
        out_specs=[WHOLE] * len(out_shape),
        out_shape=out_shape,
        scratch_shapes=[
            pltpu.VMEM((chunks, n, units, tile), BF16),
            pltpu.SemaphoreType.DMA((chunks, n)),
        ],
        cost_estimate=cost(4 * n),
    )
    return out if last else out[0]


def on_device(
    n_ctx,
    n_smp,
    n_head,
    queries,
    prefix_cache,
    suffix_cache,
    suffix_length,
    cache_sample,
    residual,
    w_out,
    norm_gain,
    gate_matrix,
    w_up,
    w_down,
):
    ctx, smp, head = (lax.axis_index(name) for name in ("ctx", "smp", "head"))
    samples = queries.shape[0]
    own_rows = residual.shape[0]
    queries = queries.reshape(samples, -1)
    prefix = prefix_cache.reshape(2, prefix_cache.shape[1], -1)
    rows, span = suffix_cache.shape[1:3]
    suffix = suffix_cache.reshape(2, rows, span, -1)
    kv_heads = prefix.shape[2] // HD
    group = QUERY_HEADS // KEY_VALUE_HEADS
    heads = kv_heads * group // n_ctx

    base = (ctx * n_smp + smp) * rows
    where = jnp.stack([ctx, smp, head, base])
    pieces = []
    for k in far_first(n_ctx) + [0]:
        piece = attention_piece(
            k, where, cache_sample, suffix_length, queries, prefix, suffix, heads, group
        )
        pieces.append(shift(piece, "ctx", n_ctx, k) if k else piece)

    parts = 2 if own_rows % 32 == 0 else 1
    step = own_rows // parts
    every = range(parts)
    others = range(1, n_smp)
    attn = merge(pieces, heads)
    gathered = [attn] + [shift(attn, "smp", n_smp, k) for k in others]
    by_head = project(where, gathered, w_out, n_ctx, n_head, own_rows, parts)
    recv = send_heads(by_head[parts:], 1)
    all_sums = [
        add_heads(by_head[p], recv, p * by_head[p].shape[0], n_ctx) for p in every
    ]
    units = gate_matrix.shape[1] // n_smp
    states, rows, full = [None] * parts, [None] * parts, [None] * parts
    received, own, hidden, theirs, acc = ([None] * parts for _ in range(5))
    sums = [None] * parts
    done = []

    def state_step(p):
        nonlocal done
        states[p], message = make_state(
            send_sums(all_sums[p]), residual[p * step : (p + 1) * step], gain, done
        )
        rows[p] = send_rows(message, n_ctx)
        done = [states[p]]

    def others_step(p):
        nonlocal done
        joined = join(rows[p], done)
        full[p] = [shift(joined, "head", n_head, b) if b else joined for b in range(n_head)]
        received[p] = []
        for k in others:
            block = (smp + k) % n_smp
            send = gate_up(block, full[p], gate_matrix, w_up, units, BF16, done)
            done = [send]
            received[p].append(shift(send, "smp", n_smp, k))

    def own_step(p):
        nonlocal done
        own[p] = gate_up(smp, full[p], gate_matrix, w_up, units, F32, done)
        done = [own[p]]

    def hidden_step(p):
        nonlocal done
        hidden[p] = activate(own[p], received[p], units, done)
        theirs[p] = [shift(hidden[p], "smp", n_smp, k) for k in others]
        done = [hidden[p]]

    blocks = [(smp + n_smp - k) % n_smp for k in range(n_smp)]

    def down_step(p, first, count, acc):
        nonlocal done
        xs = [hidden[p], *theirs[p]][first : first + count]
        last = first + count == n_smp
        out = down(blocks[first : first + count], xs, w_down, acc, last, n_head, done)
        done = [out[0] if last else out]
        return out

    gain = norm_gain[None, :]
    state_step(0)
    for p in every:
        others_step(p)
        if p + 1 < parts:
            state_step(p + 1)
            own_step(p)
            hidden_step(p)
            acc[p] = down_step(p, 0, 1, None)
            continue
        own_step(p)
        by_head = [down_step(q, 1, n_smp - 1, acc[q]) for q in range(p)]
        hidden_step(p)
        for q, (keep, *sends) in enumerate(by_head):
            sums[q] = add_heads(keep, send_heads(sends, 1), 0, n_ctx, done)
        acc[p] = down_step(p, 0, 1, None)
        outs = [finish([states[q], *send_sums(sums[q])]) for q in range(p)]
        keep, *sends = down_step(p, 1, n_smp - 1, acc[p])
    sums[-1] = add_heads(keep, send_heads(sends, PIECES), 0, n_ctx, outs)
    return finish([states[-1], *send_sums(sums[-1])], outs)


def solution(mesh):
    in_specs = (
        P(("group", "smp"), "head", None),
        P(None, ("group", "ctx"), "head", None),
        P(None, ("group", "ctx", "smp"), None, "head", None),
        P(("group", "smp")),
        P("group"),
        P(("group", "ctx", "head"), "smp"),
        P("head", "ctx", "smp"),
        P("smp"),
        P("smp", ("ctx", "head")),
        P("smp", ("ctx", "head")),
        P(("ctx", "head"), "smp"),
    )
    out_specs = P(("group", "ctx", "head"), "smp")
    body = functools.partial(
        on_device, mesh.shape["ctx"], mesh.shape["smp"], mesh.shape["head"]
    )
    return jax.shard_map(
        body, mesh=mesh, in_specs=in_specs, out_specs=out_specs, check_vma=False
    )
```

```python
import functools

import jax
import jax.numpy as jnp
from jax import lax
from jax.experimental import pallas as pl
from jax.experimental.pallas import tpu as pltpu
from jax.sharding import PartitionSpec as P

D = 8192
QUERY_HEADS = 64
KEY_VALUE_HEADS = 8
HD = 128
EPSILON = 1e-05

BF16 = jnp.bfloat16
F32 = jnp.float32
VMEM_LIMIT = 48 * 1024 * 1024
STAT_ROWS = 32
PIECES = 4
LOG2E = 1.4426950408889634
LN2 = 0.6931471805599453


def params(limit=VMEM_LIMIT):
    return pltpu.CompilerParams(vmem_limit_bytes=limit)


def cost(us):
    return pl.CostEstimate(
        flops=int(us * 1.1e9), bytes_accessed=int(us * 3.6e6), transcendentals=0
    )


IN_PLACE = pl.BlockSpec(memory_space=pl.ANY)
WHOLE = pl.BlockSpec(memory_space=pltpu.VMEM)
SCALARS = pl.BlockSpec(memory_space=pltpu.SMEM)


def run(name, kernel, in_specs, args, after=(), limit=VMEM_LIMIT, **more):
    n, m = len(args), len(after)

    def body(*refs):
        return kernel(*refs[:n], *refs[n + m :])

    return pl.pallas_call(
        body,
        name=name,
        in_specs=list(in_specs) + [IN_PLACE] * m,
        compiler_params=params(limit),
        **{"cost_estimate": cost(0.2), **more},
    )(*args, *after)


def dot(a, b):
    return jnp.dot(a, b, preferred_element_type=F32)


def dot_nt(a, b):
    return lax.dot_general(a, b, (((1,), (1,)), ((), ())), preferred_element_type=F32)


def split3(x):
    hi = x.astype(BF16).astype(F32)
    mid = (x - hi).astype(BF16).astype(F32)
    low = (x - hi - mid).astype(BF16).astype(F32)
    return hi, mid, low


def shift(x, axis, size, k):
    return lax.ppermute(x, axis, [(i, (i + k) % size) for i in range(size)])


def attention_kernel(
    heads,
    group,
    ahead,
    groups,
    where_ref,
    sample_hbm,
    length_hbm,
    q_hbm,
    prefix_hbm,
    suffix_hbm,
    msg_ref,
    sample_ref,
    length_ref,
    q_ref,
    prefix_ref,
    suffix_ref,
    number_sems,
    sems,
):
    samples = q_ref.shape[0]
    rows, span = suffix_ref.shape[1:3]
    lanes_s = rows * heads
    scale2 = HD**-0.5 * LOG2E
    n_ctx = q_hbm.shape[1] // (heads * HD)
    chunk = lax.rem(where_ref[0] + ahead, n_ctx)
    kv = lax.div(chunk * heads, group)
    q_at = pl.ds(pl.multiple_of(chunk * (heads * HD), HD), heads * HD)
    kv_at = pl.ds(pl.multiple_of(kv * HD, HD), HD)
    numbers = [
        pltpu.make_async_copy(sample_hbm, sample_ref, number_sems.at[0]),
        pltpu.make_async_copy(length_hbm, length_ref, number_sems.at[1]),
    ]
    early = [
        pltpu.make_async_copy(q_hbm.at[:, q_at], q_ref, sems.at[0]),
        pltpu.make_async_copy(prefix_hbm.at[0, :, kv_at], prefix_ref.at[0], sems.at[1]),
        pltpu.make_async_copy(prefix_hbm.at[1, :, kv_at], prefix_ref.at[1], sems.at[2]),
    ]
    late = []
    some = rows // groups
    for which in range(2):
        for g in range(groups):
            part = pl.ds(g * some, some)
            late.append(
                pltpu.make_async_copy(
                    suffix_hbm.at[which, part, :, kv_at],
                    suffix_ref.at[which, part],
                    sems.at[3 + which * groups + g],
                )
            )
    for copy in numbers + early + late:
        copy.start()

    for copy in numbers:
        copy.wait()
    column = lax.broadcasted_iota(jnp.int32, (lanes_s, 1), 0) // heads
    across = lax.broadcasted_iota(jnp.int32, (1, lanes_s), 1) // heads
    ids = jnp.zeros((lanes_s, 1), jnp.int32)
    lens = jnp.zeros((1, lanes_s), jnp.int32)
    for r in range(rows):
        sample = lax.rem(sample_ref[where_ref[3] + r], samples)
        ids = jnp.where(column == r, sample, ids)
        lens = jnp.where(across == r, length_ref[sample], lens)
    shape = (lanes_s, heads * samples)
    lane = lax.broadcasted_iota(jnp.int32, shape, 1)
    row = lax.broadcasted_iota(jnp.int32, shape, 0)
    wanted = ids + lax.rem(row, heads) * samples
    pick = jnp.where(lane == wanted, 1.0, 0.0).astype(BF16)

    early[0].wait()
    queries = jnp.concatenate(
        [q_ref[:, g * HD : (g + 1) * HD] for g in range(heads)], axis=0
    )
    early[1].wait()
    early[2].wait()
    keys = prefix_ref[0]
    values_t = prefix_ref[1].T
    pieces = []
    for g in range(heads):
        s = dot_nt(keys, queries[g * samples : (g + 1) * samples])
        high = jnp.max(s, axis=0, keepdims=True) * scale2
        weights = jnp.exp2(s * scale2 - high)
        total = jnp.sum(weights, axis=0, keepdims=True)
        pieces.append((high, total, dot(values_t, weights.astype(BF16))))

    for copy in late:
        copy.wait()
    row_queries = dot(pick, queries)
    per_tile = min(rows, max(1, 128 // heads))
    width = per_tile * heads
    outs, lses = [], []
    for tile in range(rows // per_tile):
        at = tile * per_tile
        q_tile = row_queries[at * heads : at * heads + width]
        own = lax.broadcasted_iota(jnp.int32, (width, HD), 0) // heads
        q_wide = jnp.concatenate(
            [jnp.where(own == r, q_tile, 0.0).astype(BF16) for r in range(per_tile)], axis=1
        )
        row_keys = jnp.concatenate(
            [suffix_ref[0, at + r] for r in range(per_tile)], axis=1
        )
        s = dot_nt(row_keys, q_wide) * scale2
        t = lax.broadcasted_iota(jnp.int32, s.shape, 0)
        s = jnp.where(t < lens[:, at * heads : at * heads + width], s, -jnp.inf)
        high = jnp.max(s, axis=0, keepdims=True)
        weights = jnp.exp2(s - high)
        total = jnp.sum(weights, axis=0, keepdims=True)
        turned = weights.T
        own_t = lax.broadcasted_iota(jnp.int32, (width, span), 0) // heads
        w_wide = jnp.concatenate(
            [jnp.where(own_t == r, turned, 0.0).astype(BF16) for r in range(per_tile)], axis=1
        )
        values = suffix_ref[1, at : at + per_tile].reshape(per_tile * span, HD)
        outs.append(dot(w_wide, values).T / total)
        lses.append(high + jnp.log2(total))
    hi, mid, low = split3(jnp.concatenate(lses, axis=1))
    sub = lax.broadcasted_iota(jnp.int32, (16, lanes_s), 0)
    stats = jnp.where(sub == 0, hi, jnp.where(sub == 1, mid, jnp.where(sub == 2, low, 1.0)))
    to_place = jnp.concatenate([jnp.concatenate(outs, axis=1), stats], axis=0).astype(BF16)
    placed = dot(to_place, pick)
    placed_lse = placed[HD : HD + 1] + placed[HD + 1 : HD + 2] + placed[HD + 2 : HD + 3]
    present = placed[HD + 3 : HD + 4]

    rows_out = []
    for g, (high, total, out) in enumerate(pieces):
        at = slice(g * samples, (g + 1) * samples)
        here = present[:, at] > 0.5
        other = jnp.where(here, placed_lse[:, at], high)
        top = jnp.maximum(high, other)
        own_weight = jnp.exp2(high - top)
        other_weight = jnp.where(here, jnp.exp2(other - top), 0.0)
        both = own_weight * total + other_weight
        out = out * (own_weight / both) + placed[:HD, at] * (other_weight / both)
        msg_ref[g * HD : (g + 1) * HD, :] = out.astype(BF16)
        rows_out.append(top + jnp.log2(both))
    sub = lax.broadcasted_iota(jnp.int32, (STAT_ROWS, samples), 0)
    stats = jnp.zeros((STAT_ROWS, samples), F32)
    for g in range(heads):
        for part, value in enumerate(split3(rows_out[g])):
            stats = jnp.where(sub == part * heads + g, value, stats)
    msg_ref[heads * HD :, :] = stats.astype(BF16)


def attention_piece(
    ahead, where, cache_sample, suffix_length, queries, prefix, suffix, heads, group
):
    samples = queries.shape[0]
    block, rows, span = prefix.shape[1], suffix.shape[1], suffix.shape[2]
    groups = 4 if rows % 4 == 0 else 1
    return run(
        "attention",
        functools.partial(attention_kernel, heads, group, ahead, groups),
        [SCALARS] + [IN_PLACE] * 5,
        [where, cache_sample, suffix_length, queries, prefix, suffix],
        out_specs=WHOLE,
        out_shape=jax.ShapeDtypeStruct((heads * HD + STAT_ROWS, samples), BF16),
        scratch_shapes=[
            pltpu.SMEM(cache_sample.shape, jnp.int32),
            pltpu.SMEM(suffix_length.shape, jnp.int32),
            pltpu.VMEM((samples, heads * HD), BF16),
            pltpu.VMEM((2, block, HD), BF16),
            pltpu.VMEM((2, rows, span, HD), BF16),
            pltpu.SemaphoreType.DMA((2,)),
            pltpu.SemaphoreType.DMA((3 + 2 * groups,)),
        ],
        cost_estimate=cost(5),
        limit=60 * 1024 * 1024,
    )


def merge_kernel(heads, *refs):
    pieces, out_ref = refs[:-1], refs[-1]
    top_rows = heads * HD
    lses = []
    for ref in pieces:
        stats = ref[top_rows:, :].astype(F32)
        lses.append(
            stats[:heads] + stats[heads : 2 * heads] + stats[2 * heads : 3 * heads]
        )
    top = functools.reduce(jnp.maximum, lses)
    weights = [jnp.exp2(lse - top) for lse in lses]
    denom = functools.reduce(jnp.add, weights)
    weights = [w / denom for w in weights]
    for g in range(heads):
        total = None
        for ref, w in zip(pieces, weights):
            term = ref[g * HD : (g + 1) * HD, :].astype(F32) * w[g : g + 1]
            total = term if total is None else total + term
        out_ref[:, g * HD : (g + 1) * HD] = total.T.astype(BF16)


def merge(pieces, heads):
    samples = pieces[0].shape[1]
    return run(
        "merge",
        functools.partial(merge_kernel, heads),
        [WHOLE] * len(pieces),
        pieces,
        out_specs=WHOLE,
        out_shape=jax.ShapeDtypeStruct((samples, heads * HD), BF16),
        cost_estimate=cost(1.3),
    )


def proj_kernel(n_ctx, n_head, own_rows, n_smp, parts, chunks, where_ref, *refs):
    attn_refs, w_hbm, refs = refs[:n_smp], refs[n_smp], refs[n_smp + 1 :]
    out_refs, (full, lhs, w_buf, sems) = refs[:-4], refs[-4:]
    ctx, smp, head = where_ref[0], where_ref[1], where_ref[2]
    samples = attn_refs[0].shape[0]
    tile = w_buf.shape[2]
    copies = [
        pltpu.make_async_copy(
            w_hbm.at[0, :, pl.ds(i * tile, tile)], w_buf.at[i], sems.at[i]
        )
        for i in range(chunks)
    ]
    for copy in copies:
        copy.start()
    for k, ref in enumerate(attn_refs):
        at = lax.rem(smp + n_smp - k, n_smp) * samples
        full[pl.ds(pl.multiple_of(at, 16), samples), :] = ref[...]
    step = own_rows // parts
    to = 0
    for b in range(n_head):
        h = lax.rem(head + b, n_head)
        for p in range(parts):
            for t in range(n_ctx):
                c = lax.rem(ctx + n_ctx - t, n_ctx)
                at = (c * n_head + h) * own_rows + p * step
                lhs[to : to + step, :] = full[pl.ds(pl.multiple_of(at, step), step), :]
                to += step
    for i, copy in enumerate(copies):
        copy.wait()
        out = dot(lhs[...], w_buf[i]).astype(BF16)
        row = 0
        for ref in out_refs:
            ref[:, i * tile : (i + 1) * tile] = out[row : row + ref.shape[0]]
            row += ref.shape[0]


def project(where, attn, w_out, n_ctx, n_head, own_rows, parts):
    n_smp = len(attn)
    samples, depth = attn[0].shape
    width = w_out.shape[2]
    chunks = 4
    tile = width // chunks
    per = n_ctx * own_rows // parts
    rows = per * parts * n_head
    return run(
        "project",
        functools.partial(proj_kernel, n_ctx, n_head, own_rows, n_smp, parts, chunks),
        [SCALARS] + [WHOLE] * n_smp + [IN_PLACE],
        [where, *attn, w_out],
        out_specs=[WHOLE] * (parts + n_head - 1),
        out_shape=[jax.ShapeDtypeStruct((per, width), BF16)] * parts
        + [jax.ShapeDtypeStruct((per * parts, width), BF16)] * (n_head - 1),
        scratch_shapes=[
            pltpu.VMEM((n_smp * samples, depth), BF16),
            pltpu.VMEM((rows, depth), BF16),
            pltpu.VMEM((chunks, depth, tile), BF16),
            pltpu.SemaphoreType.DMA((chunks,)),
        ],
        cost_estimate=cost(5),
    )


def add_heads_kernel(n_ctx, row, keep_ref, *refs):
    recv, outs = refs[:-n_ctx], refs[-n_ctx:]
    rows, width = outs[0].shape[0], recv[0].shape[1]
    pieces = outs[0].shape[1] // width
    for t, ref in enumerate(outs):
        for j in range(pieces):
            columns = slice(j * width, (j + 1) * width)
            total = keep_ref[t * rows : (t + 1) * rows, columns].astype(F32)
            for other in recv[j::pieces]:
                at = row + t * rows
                total = total + other[at : at + rows].astype(F32)
            ref[:, columns] = total.astype(BF16)


def send_heads(sends, pieces):
    step = sends[0].shape[1] // pieces
    return [
        shift(send[:, j * step : (j + 1) * step], "head", len(sends) + 1, b)
        for b, send in enumerate(sends, 1)
        for j in range(pieces)
    ]


def add_heads(keep, recv, row, n_ctx, after=()):
    rows, width = keep.shape
    return run(
        "add_heads",
        functools.partial(add_heads_kernel, n_ctx, row),
        [WHOLE] * (1 + len(recv)),
        [keep, *recv],
        after,
        out_specs=[WHOLE] * n_ctx,
        out_shape=[jax.ShapeDtypeStruct((rows // n_ctx, width), BF16)] * n_ctx,
    )


def far_first(n):
    return sorted(range(1, n), key=lambda k: -min(k, n - k))


def send_sums(sums):
    n_ctx = len(sums)
    return [sums[0]] + [shift(sums[t], "ctx", n_ctx, -t) for t in far_first(n_ctx)]


def send_rows(x, n_ctx):
    got = {t: shift(x, "ctx", n_ctx, t) for t in far_first(n_ctx)}
    return [x] + [got[t] for t in range(1, n_ctx)]


def join_kernel(*refs):
    pieces, out_ref = refs[:-1], refs[-1]
    rows = pieces[0].shape[0]
    for t, ref in enumerate(pieces):
        out_ref[t * rows : (t + 1) * rows, :] = ref[...]


def join(pieces, after):
    rows, width = pieces[0].shape
    return run(
        "join",
        join_kernel,
        [WHOLE] * len(pieces),
        pieces,
        after,
        out_specs=WHOLE,
        out_shape=jax.ShapeDtypeStruct((rows * len(pieces), width), BF16),
    )


def state_kernel(n_pieces, *refs):
    pieces, (res_ref, gain_ref, state_ref, msg_ref) = refs[:n_pieces], refs[n_pieces:]
    width = res_ref.shape[1]
    total = res_ref[...].astype(F32)
    for ref in pieces:
        total = total + ref[...].astype(F32)
    state = total.astype(BF16)
    state_ref[...] = state
    wide = state.astype(F32)
    msg_ref[:, :width] = (wide * gain_ref[...]).astype(BF16)
    hi, mid, low = split3(jnp.sum(wide * wide, axis=1, keepdims=True))
    lane = lax.broadcasted_iota(jnp.int32, (hi.shape[0], HD), 1)
    stats = jnp.where(
        lane == 0, hi, jnp.where(lane == 1, mid, jnp.where(lane == 2, low, 0.0))
    )
    msg_ref[:, width:] = stats.astype(BF16)


def make_state(pieces, residual, gain, after):
    rows, width = residual.shape
    return run(
        "state",
        functools.partial(state_kernel, len(pieces)),
        [WHOLE] * (len(pieces) + 2),
        [*pieces, residual, gain],
        after,
        out_specs=[WHOLE] * 2,
        out_shape=[
            jax.ShapeDtypeStruct((rows, width), BF16),
            jax.ShapeDtypeStruct((rows, width + HD), BF16),
        ],
        cost_estimate=cost(8),
    )


def finish_kernel(above, *refs):
    terms, out_ref = refs[above:-1], refs[-1]
    total = terms[0][...].astype(F32)
    for ref in terms[1:]:
        total = total + ref[...].astype(F32)
    row = 0
    for ref in refs[:above]:
        out_ref[row : row + ref.shape[0], :] = ref[...]
        row += ref.shape[0]
    out_ref[row:, :] = total.astype(out_ref.dtype)


def finish(pieces, above=()):
    total = pieces[-1]
    for i in reversed(range(len(pieces) - 1)):
        on_top = list(above) if i == 0 else []
        rows, width = total.shape
        shape = (sum(x.shape[0] for x in on_top) + rows, width)
        total = run(
            "finish",
            functools.partial(finish_kernel, len(on_top)),
            [WHOLE] * (len(on_top) + 2),
            [*on_top, total, pieces[i]],
            out_specs=WHOLE,
            out_shape=jax.ShapeDtypeStruct(shape, F32 if i else BF16),
        )
    return total


def gate_up_kernel(chunks, n_parts, where_ref, *refs):
    parts, (g_hbm, u_hbm, out_ref, x, acc, g_buf, u_buf, g_sem, u_sem) = (
        refs[:n_parts],
        refs[n_parts:],
    )
    tile, units = g_buf.shape[1:]
    at = pl.multiple_of(where_ref[0] * units, 128)

    def chunk_copy(i, which):
        hbm, buf, sem = ((g_hbm, g_buf, g_sem), (u_hbm, u_buf, u_sem))[which]
        from_at = pl.multiple_of(i * tile, tile)
        return pltpu.make_async_copy(
            hbm.at[pl.ds(from_at, tile), pl.ds(at, units)], buf.at[i], sem.at[i]
        )

    for i in range(chunks):
        chunk_copy(i, 0).start()
        chunk_copy(i, 1).start()
    row = 0
    for ref in parts:
        x[row : row + ref.shape[0]] = ref[:, : x.shape[1]]
        row += ref.shape[0]
    acc[...] = jnp.zeros_like(acc)
    turns = 2

    @pl.loop(0, turns)
    def _(turn):
        gate = up = None
        for j in range(chunks // turns):
            i = turn * (chunks // turns) + j
            lhs = x[:, pl.ds(pl.multiple_of(i * tile, tile), tile)]
            chunk_copy(i, 0).wait()
            term = dot(lhs, g_buf[i])
            gate = term if gate is None else gate + term
            chunk_copy(i, 1).wait()
            term = dot(lhs, u_buf[i])
            up = term if up is None else up + term
        acc[:, :units] += gate
        acc[:, units:] += up

    out_ref[:, : 2 * units] = acc[...].astype(out_ref.dtype)
    row = 0
    for ref in parts:
        out_ref[row : row + ref.shape[0], 2 * units :] = ref[:, x.shape[1] :].astype(
            out_ref.dtype
        )
        row += ref.shape[0]


def gate_up(block, parts, gate_matrix, w_up, units, dtype, after=()):
    rows, depth = sum(p.shape[0] for p in parts), gate_matrix.shape[0]
    chunks = 8
    tile = depth // chunks
    return run(
        "gate_up",
        functools.partial(gate_up_kernel, chunks, len(parts)),
        [SCALARS] + [WHOLE] * len(parts) + [IN_PLACE] * 2,
        [block.reshape(1), *parts, gate_matrix, w_up],
        after,
        out_specs=WHOLE,
        out_shape=jax.ShapeDtypeStruct((rows, 2 * units + HD), dtype),
        scratch_shapes=[pltpu.VMEM((rows, depth), BF16), pltpu.VMEM((rows, 2 * units), F32)]
        + [pltpu.VMEM((chunks, tile, units), BF16)] * 2
        + [pltpu.SemaphoreType.DMA((chunks,))] * 2,
        cost_estimate=cost(6 if dtype == BF16 else 1),
    )


def act_kernel(own_ref, *refs):
    recv, out_ref = refs[:-1], refs[-1]
    total = own_ref[...]
    for ref in recv:
        total = total + ref[...].astype(F32)
    units = out_ref.shape[1]
    square = jnp.sum(total[:, 2 * units :], axis=1, keepdims=True)
    factor = lax.rsqrt(square / D + EPSILON)
    gate = factor * total[:, :units]
    up = factor * total[:, units : 2 * units]
    out_ref[...] = (gate / (1.0 + jnp.exp(-gate)) * up).astype(BF16)


def activate(own, recv, units, after):
    return run(
        "activate",
        act_kernel,
        [WHOLE] * (1 + len(recv)),
        [own, *recv],
        after,
        out_specs=WHOLE,
        out_shape=jax.ShapeDtypeStruct((own.shape[0], units), BF16),
    )


def down_kernel(n_parts, chunks, has_acc, last, n_head, where_ref, *refs):
    xs, refs = refs[:n_parts], refs[n_parts:]
    if has_acc:
        acc_ref, w_hbm, *outs, w_buf, sems = refs
    else:
        w_hbm, *outs, w_buf, sems = refs
    units, tile = w_buf.shape[2:]
    copies = []
    for i in range(chunks):
        for p in range(n_parts):
            at = pl.multiple_of(where_ref[p] * units, 16)
            copies.append(
                pltpu.make_async_copy(
                    w_hbm.at[pl.ds(at, units), pl.ds(i * tile, tile)],
                    w_buf.at[i, p],
                    sems.at[i, p],
                )
            )
    for copy in copies:
        copy.start()
    for i in range(chunks):
        total = acc_ref[:, i * tile : (i + 1) * tile] if has_acc else None
        for p in range(n_parts):
            copies[i * n_parts + p].wait()
            term = dot(xs[p][...], w_buf[i, p])
            total = term if total is None else total + term
        if last:
            per = total.shape[0] // n_head
            for b in range(n_head):
                outs[b][:, i * tile : (i + 1) * tile] = total[
                    b * per : (b + 1) * per
                ].astype(BF16)
        else:
            outs[0][:, i * tile : (i + 1) * tile] = total


def down(blocks, xs, w_down, acc, last, n_head, after):
    rows, units = xs[0].shape
    width = w_down.shape[1]
    chunks = 8
    tile = width // chunks
    n = len(xs)
    args = list(xs) + ([] if acc is None else [acc])
    if last:
        out_shape = [jax.ShapeDtypeStruct((rows // n_head, width), BF16)] * n_head
    else:
        out_shape = [jax.ShapeDtypeStruct((rows, width), F32)]
    out = run(
        "down",
        functools.partial(down_kernel, n, chunks, acc is not None, last, n_head),
        [SCALARS] + [WHOLE] * len(args) + [IN_PLACE],
        [jnp.stack(blocks), *args, w_down],
        after,
        out_specs=[WHOLE] * len(out_shape),
        out_shape=out_shape,
        scratch_shapes=[
            pltpu.VMEM((chunks, n, units, tile), BF16),
            pltpu.SemaphoreType.DMA((chunks, n)),
        ],
        cost_estimate=cost(4 * n),
    )
    return out if last else out[0]


def on_device(
    n_ctx,
    n_smp,
    n_head,
    queries,
    prefix_cache,
    suffix_cache,
    suffix_length,
    cache_sample,
    residual,
    w_out,
    norm_gain,
    gate_matrix,
    w_up,
    w_down,
):
    ctx, smp, head = (lax.axis_index(name) for name in ("ctx", "smp", "head"))
    samples = queries.shape[0]
    own_rows = residual.shape[0]
    queries = queries.reshape(samples, -1)
    prefix = prefix_cache.reshape(2, prefix_cache.shape[1], -1)
    rows, span = suffix_cache.shape[1:3]
    suffix = suffix_cache.reshape(2, rows, span, -1)
    kv_heads = prefix.shape[2] // HD
    group = QUERY_HEADS // KEY_VALUE_HEADS
    heads = kv_heads * group // n_ctx

    base = (ctx * n_smp + smp) * rows
    where = jnp.stack([ctx, smp, head, base])
    pieces = []
    for k in far_first(n_ctx) + [0]:
        piece = attention_piece(
            k, where, cache_sample, suffix_length, queries, prefix, suffix, heads, group
        )
        pieces.append(shift(piece, "ctx", n_ctx, k) if k else piece)

    parts = 2 if own_rows % 32 == 0 else 1
    step = own_rows // parts
    every = range(parts)
    others = range(1, n_smp)
    attn = merge(pieces, heads)
    gathered = [attn] + [shift(attn, "smp", n_smp, k) for k in others]
    by_head = project(where, gathered, w_out, n_ctx, n_head, own_rows, parts)
    all_sums = []
    for p in every:
        per = by_head[p].shape[0]
        sends = [x[p * per : (p + 1) * per] for x in by_head[parts:]]
        all_sums.append(add_heads(by_head[p], send_heads(sends, 1), 0, n_ctx))
    units = gate_matrix.shape[1] // n_smp
    states, rows, full = [None] * parts, [None] * parts, [None] * parts
    received, own, hidden, theirs, acc = ([None] * parts for _ in range(5))
    sums = [None] * parts
    done = []

    def state_step(p):
        nonlocal done
        states[p], message = make_state(
            send_sums(all_sums[p]), residual[p * step : (p + 1) * step], gain, done
        )
        rows[p] = send_rows(message, n_ctx)
        done = [states[p]]

    def others_step(p):
        nonlocal done
        joined = join(rows[p], done)
        full[p] = [shift(joined, "head", n_head, b) if b else joined for b in range(n_head)]
        received[p] = []
        for k in others:
            block = (smp + k) % n_smp
            send = gate_up(block, full[p], gate_matrix, w_up, units, BF16, done)
            done = [send]
            received[p].append(shift(send, "smp", n_smp, k))

    def own_step(p):
        nonlocal done
        own[p] = gate_up(smp, full[p], gate_matrix, w_up, units, F32, done)
        done = [own[p]]

    def hidden_step(p):
        nonlocal done
        hidden[p] = activate(own[p], received[p], units, done)
        theirs[p] = [shift(hidden[p], "smp", n_smp, k) for k in others]
        done = [hidden[p]]

    blocks = [(smp + n_smp - k) % n_smp for k in range(n_smp)]

    def down_step(p, first, count, acc):
        nonlocal done
        xs = [hidden[p], *theirs[p]][first : first + count]
        last = first + count == n_smp
        out = down(blocks[first : first + count], xs, w_down, acc, last, n_head, done)
        done = [out[0] if last else out]
        return out

    gain = norm_gain[None, :]
    state_step(0)
    for p in every:
        others_step(p)
        if p + 1 < parts:
            state_step(p + 1)
            own_step(p)
            hidden_step(p)
            acc[p] = down_step(p, 0, 1, None)
            continue
        own_step(p)
        by_head = [down_step(q, 1, n_smp - 1, acc[q]) for q in range(p)]
        hidden_step(p)
        for q, (keep, *sends) in enumerate(by_head):
            sums[q] = add_heads(keep, send_heads(sends, 1), 0, n_ctx, done)
        acc[p] = down_step(p, 0, 1, None)
        outs = [finish([states[q], *send_sums(sums[q])]) for q in range(p)]
        keep, *sends = down_step(p, 1, n_smp - 1, acc[p])
    sums[-1] = add_heads(keep, send_heads(sends, PIECES), 0, n_ctx, outs)
    return finish([states[-1], *send_sums(sums[-1])], outs)


def solution(mesh):
    in_specs = (
        P(("group", "smp"), "head", None),
        P(None, ("group", "ctx"), "head", None),
        P(None, ("group", "ctx", "smp"), None, "head", None),
        P(("group", "smp")),
        P("group"),
        P(("group", "ctx", "head"), "smp"),
        P("head", "ctx", "smp"),
        P("smp"),
        P("smp", ("ctx", "head")),
        P("smp", ("ctx", "head")),
        P(("ctx", "head"), "smp"),
    )
    out_specs = P(("group", "ctx", "head"), "smp")
    body = functools.partial(
        on_device, mesh.shape["ctx"], mesh.shape["smp"], mesh.shape["head"]
    )
    return jax.shard_map(
        body, mesh=mesh, in_specs=in_specs, out_specs=out_specs, check_vma=False
    )
```

```python
import functools

import jax
import jax.numpy as jnp
from jax import lax
from jax.experimental import pallas as pl
from jax.experimental.pallas import tpu as pltpu
from jax.sharding import PartitionSpec as P

D = 8192
QUERY_HEADS = 64
KEY_VALUE_HEADS = 8
HD = 128
EPSILON = 1e-05

BF16 = jnp.bfloat16
F32 = jnp.float32
VMEM_LIMIT = 48 * 1024 * 1024
STAT_ROWS = 32
PIECES = 4
LOG2E = 1.4426950408889634
LN2 = 0.6931471805599453


def params(limit=VMEM_LIMIT):
    return pltpu.CompilerParams(vmem_limit_bytes=limit)


def cost(us):
    return pl.CostEstimate(
        flops=int(us * 1.1e9), bytes_accessed=int(us * 3.6e6), transcendentals=0
    )


IN_PLACE = pl.BlockSpec(memory_space=pl.ANY)
WHOLE = pl.BlockSpec(memory_space=pltpu.VMEM)
SCALARS = pl.BlockSpec(memory_space=pltpu.SMEM)


def run(name, kernel, in_specs, args, after=(), limit=VMEM_LIMIT, **more):
    n, m = len(args), len(after)

    def body(*refs):
        return kernel(*refs[:n], *refs[n + m :])

    return pl.pallas_call(
        body,
        name=name,
        in_specs=list(in_specs) + [IN_PLACE] * m,
        compiler_params=params(limit),
        **{"cost_estimate": cost(0.2), **more},
    )(*args, *after)


def dot(a, b):
    return jnp.dot(a, b, preferred_element_type=F32)


def dot_nt(a, b):
    return lax.dot_general(a, b, (((1,), (1,)), ((), ())), preferred_element_type=F32)


def split3(x):
    hi = x.astype(BF16).astype(F32)
    mid = (x - hi).astype(BF16).astype(F32)
    low = (x - hi - mid).astype(BF16).astype(F32)
    return hi, mid, low


def shift(x, axis, size, k):
    return lax.ppermute(x, axis, [(i, (i + k) % size) for i in range(size)])


def attention_kernel(
    heads,
    group,
    ahead,
    groups,
    where_ref,
    sample_hbm,
    length_hbm,
    q_hbm,
    prefix_hbm,
    suffix_hbm,
    msg_ref,
    sample_ref,
    length_ref,
    q_ref,
    prefix_ref,
    suffix_ref,
    number_sems,
    sems,
):
    samples = q_ref.shape[0]
    rows, span = suffix_ref.shape[1:3]
    lanes_s = rows * heads
    scale2 = HD**-0.5 * LOG2E
    n_ctx = q_hbm.shape[1] // (heads * HD)
    chunk = lax.rem(where_ref[0] + ahead, n_ctx)
    kv = lax.div(chunk * heads, group)
    q_at = pl.ds(pl.multiple_of(chunk * (heads * HD), HD), heads * HD)
    kv_at = pl.ds(pl.multiple_of(kv * HD, HD), HD)
    numbers = [
        pltpu.make_async_copy(sample_hbm, sample_ref, number_sems.at[0]),
        pltpu.make_async_copy(length_hbm, length_ref, number_sems.at[1]),
    ]
    early = [
        pltpu.make_async_copy(q_hbm.at[:, q_at], q_ref, sems.at[0]),
        pltpu.make_async_copy(prefix_hbm.at[0, :, kv_at], prefix_ref.at[0], sems.at[1]),
        pltpu.make_async_copy(prefix_hbm.at[1, :, kv_at], prefix_ref.at[1], sems.at[2]),
    ]
    late = []
    some = rows // groups
    for which in range(2):
        for g in range(groups):
            part = pl.ds(g * some, some)
            late.append(
                pltpu.make_async_copy(
                    suffix_hbm.at[which, part, :, kv_at],
                    suffix_ref.at[which, part],
                    sems.at[3 + which * groups + g],
                )
            )
    for copy in numbers + early + late:
        copy.start()

    for copy in numbers:
        copy.wait()
    column = lax.broadcasted_iota(jnp.int32, (lanes_s, 1), 0) // heads
    across = lax.broadcasted_iota(jnp.int32, (1, lanes_s), 1) // heads
    ids = jnp.zeros((lanes_s, 1), jnp.int32)
    lens = jnp.zeros((1, lanes_s), jnp.int32)
    for r in range(rows):
        sample = lax.rem(sample_ref[where_ref[3] + r], samples)
        ids = jnp.where(column == r, sample, ids)
        lens = jnp.where(across == r, length_ref[sample], lens)
    shape = (lanes_s, heads * samples)
    lane = lax.broadcasted_iota(jnp.int32, shape, 1)
    row = lax.broadcasted_iota(jnp.int32, shape, 0)
    wanted = ids + lax.rem(row, heads) * samples
    pick = jnp.where(lane == wanted, 1.0, 0.0).astype(BF16)

    early[0].wait()
    queries = jnp.concatenate(
        [q_ref[:, g * HD : (g + 1) * HD] for g in range(heads)], axis=0
    )
    early[1].wait()
    early[2].wait()
    keys = prefix_ref[0]
    values_t = prefix_ref[1].T
    pieces = []
    for g in range(heads):
        s = dot_nt(keys, queries[g * samples : (g + 1) * samples])
        high = jnp.max(s, axis=0, keepdims=True) * scale2
        weights = jnp.exp2(s * scale2 - high)
        total = jnp.sum(weights, axis=0, keepdims=True)
        pieces.append((high, total, dot(values_t, weights.astype(BF16))))

    for copy in late:
        copy.wait()
    row_queries = dot(pick, queries)
    per_tile = min(rows, max(1, 128 // heads))
    width = per_tile * heads
    outs, lses = [], []
    for tile in range(rows // per_tile):
        at = tile * per_tile
        q_tile = row_queries[at * heads : at * heads + width]
        own = lax.broadcasted_iota(jnp.int32, (width, HD), 0) // heads
        q_wide = jnp.concatenate(
            [jnp.where(own == r, q_tile, 0.0).astype(BF16) for r in range(per_tile)], axis=1
        )
        row_keys = jnp.concatenate(
            [suffix_ref[0, at + r] for r in range(per_tile)], axis=1
        )
        s = dot_nt(row_keys, q_wide) * scale2
        t = lax.broadcasted_iota(jnp.int32, s.shape, 0)
        s = jnp.where(t < lens[:, at * heads : at * heads + width], s, -jnp.inf)
        high = jnp.max(s, axis=0, keepdims=True)
        weights = jnp.exp2(s - high)
        total = jnp.sum(weights, axis=0, keepdims=True)
        turned = weights.T
        own_t = lax.broadcasted_iota(jnp.int32, (width, span), 0) // heads
        w_wide = jnp.concatenate(
            [jnp.where(own_t == r, turned, 0.0).astype(BF16) for r in range(per_tile)], axis=1
        )
        values = suffix_ref[1, at : at + per_tile].reshape(per_tile * span, HD)
        outs.append(dot(w_wide, values).T / total)
        lses.append(high + jnp.log2(total))
    hi, mid, low = split3(jnp.concatenate(lses, axis=1))
    sub = lax.broadcasted_iota(jnp.int32, (16, lanes_s), 0)
    stats = jnp.where(sub == 0, hi, jnp.where(sub == 1, mid, jnp.where(sub == 2, low, 1.0)))
    to_place = jnp.concatenate([jnp.concatenate(outs, axis=1), stats], axis=0).astype(BF16)
    placed = dot(to_place, pick)
    placed_lse = placed[HD : HD + 1] + placed[HD + 1 : HD + 2] + placed[HD + 2 : HD + 3]
    present = placed[HD + 3 : HD + 4]

    rows_out = []
    for g, (high, total, out) in enumerate(pieces):
        at = slice(g * samples, (g + 1) * samples)
        here = present[:, at] > 0.5
        other = jnp.where(here, placed_lse[:, at], high)
        top = jnp.maximum(high, other)
        own_weight = jnp.exp2(high - top)
        other_weight = jnp.where(here, jnp.exp2(other - top), 0.0)
        both = own_weight * total + other_weight
        out = out * (own_weight / both) + placed[:HD, at] * (other_weight / both)
        msg_ref[g * HD : (g + 1) * HD, :] = out.astype(BF16)
        rows_out.append(top + jnp.log2(both))
    sub = lax.broadcasted_iota(jnp.int32, (STAT_ROWS, samples), 0)
    stats = jnp.zeros((STAT_ROWS, samples), F32)
    for g in range(heads):
        for part, value in enumerate(split3(rows_out[g])):
            stats = jnp.where(sub == part * heads + g, value, stats)
    msg_ref[heads * HD :, :] = stats.astype(BF16)


def attention_piece(
    ahead, where, cache_sample, suffix_length, queries, prefix, suffix, heads, group
):
    samples = queries.shape[0]
    block, rows, span = prefix.shape[1], suffix.shape[1], suffix.shape[2]
    groups = 4 if rows % 4 == 0 else 1
    return run(
        "attention",
        functools.partial(attention_kernel, heads, group, ahead, groups),
        [SCALARS] + [IN_PLACE] * 5,
        [where, cache_sample, suffix_length, queries, prefix, suffix],
        out_specs=WHOLE,
        out_shape=jax.ShapeDtypeStruct((heads * HD + STAT_ROWS, samples), BF16),
        scratch_shapes=[
            pltpu.SMEM(cache_sample.shape, jnp.int32),
            pltpu.SMEM(suffix_length.shape, jnp.int32),
            pltpu.VMEM((samples, heads * HD), BF16),
            pltpu.VMEM((2, block, HD), BF16),
            pltpu.VMEM((2, rows, span, HD), BF16),
            pltpu.SemaphoreType.DMA((2,)),
            pltpu.SemaphoreType.DMA((3 + 2 * groups,)),
        ],
        cost_estimate=cost(5),
        limit=60 * 1024 * 1024,
    )


def merge_kernel(heads, *refs):
    pieces, out_ref = refs[:-1], refs[-1]
    top_rows = heads * HD
    lses = []
    for ref in pieces:
        stats = ref[top_rows:, :].astype(F32)
        lses.append(
            stats[:heads] + stats[heads : 2 * heads] + stats[2 * heads : 3 * heads]
        )
    top = functools.reduce(jnp.maximum, lses)
    weights = [jnp.exp2(lse - top) for lse in lses]
    denom = functools.reduce(jnp.add, weights)
    weights = [w / denom for w in weights]
    for g in range(heads):
        total = None
        for ref, w in zip(pieces, weights):
            term = ref[g * HD : (g + 1) * HD, :].astype(F32) * w[g : g + 1]
            total = term if total is None else total + term
        out_ref[:, g * HD : (g + 1) * HD] = total.T.astype(BF16)


def merge(pieces, heads):
    samples = pieces[0].shape[1]
    return run(
        "merge",
        functools.partial(merge_kernel, heads),
        [WHOLE] * len(pieces),
        pieces,
        out_specs=WHOLE,
        out_shape=jax.ShapeDtypeStruct((samples, heads * HD), BF16),
        cost_estimate=cost(1.3),
    )


def proj_kernel(n_ctx, n_head, own_rows, n_smp, parts, chunks, where_ref, *refs):
    attn_refs, w_hbm, refs = refs[:n_smp], refs[n_smp], refs[n_smp + 1 :]
    out_refs, (full, lhs, w_buf, sems) = refs[:-4], refs[-4:]
    ctx, smp, head = where_ref[0], where_ref[1], where_ref[2]
    samples = attn_refs[0].shape[0]
    tile = w_buf.shape[2]
    copies = [
        pltpu.make_async_copy(
            w_hbm.at[0, :, pl.ds(i * tile, tile)], w_buf.at[i], sems.at[i]
        )
        for i in range(chunks)
    ]
    for copy in copies:
        copy.start()
    for k, ref in enumerate(attn_refs):
        at = lax.rem(smp + n_smp - k, n_smp) * samples
        full[pl.ds(pl.multiple_of(at, 16), samples), :] = ref[...]
    step = own_rows // parts
    to = 0
    for b in range(n_head):
        h = lax.rem(head + b, n_head)
        for p in range(parts):
            for t in range(n_ctx):
                c = lax.rem(ctx + n_ctx - t, n_ctx)
                at = (c * n_head + h) * own_rows + p * step
                lhs[to : to + step, :] = full[pl.ds(pl.multiple_of(at, step), step), :]
                to += step
    for i, copy in enumerate(copies):
        copy.wait()
        out = dot(lhs[...], w_buf[i]).astype(BF16)
        row = 0
        for ref in out_refs:
            ref[:, i * tile : (i + 1) * tile] = out[row : row + ref.shape[0]]
            row += ref.shape[0]


def project(where, attn, w_out, n_ctx, n_head, own_rows, parts):
    n_smp = len(attn)
    samples, depth = attn[0].shape
    width = w_out.shape[2]
    chunks = 8
    tile = width // chunks
    per = n_ctx * own_rows // parts
    rows = per * parts * n_head
    return run(
        "project",
        functools.partial(proj_kernel, n_ctx, n_head, own_rows, n_smp, parts, chunks),
        [SCALARS] + [WHOLE] * n_smp + [IN_PLACE],
        [where, *attn, w_out],
        out_specs=[WHOLE] * (parts + n_head - 1),
        out_shape=[jax.ShapeDtypeStruct((per, width), BF16)] * parts
        + [jax.ShapeDtypeStruct((per * parts, width), BF16)] * (n_head - 1),
        scratch_shapes=[
            pltpu.VMEM((n_smp * samples, depth), BF16),
            pltpu.VMEM((rows, depth), BF16),
            pltpu.VMEM((chunks, depth, tile), BF16),
            pltpu.SemaphoreType.DMA((chunks,)),
        ],
        cost_estimate=cost(5),
    )


def add_heads_kernel(n_ctx, row, keep_ref, *refs):
    recv, outs = refs[:-n_ctx], refs[-n_ctx:]
    rows, width = outs[0].shape[0], recv[0].shape[1]
    pieces = outs[0].shape[1] // width
    for t, ref in enumerate(outs):
        for j in range(pieces):
            columns = slice(j * width, (j + 1) * width)
            total = keep_ref[t * rows : (t + 1) * rows, columns].astype(F32)
            for other in recv[j::pieces]:
                at = row + t * rows
                total = total + other[at : at + rows].astype(F32)
            ref[:, columns] = total.astype(BF16)


def send_heads(sends, pieces):
    step = sends[0].shape[1] // pieces
    return [
        shift(send[:, j * step : (j + 1) * step], "head", len(sends) + 1, b)
        for b, send in enumerate(sends, 1)
        for j in range(pieces)
    ]


def add_heads(keep, recv, row, n_ctx, after=()):
    rows, width = keep.shape
    return run(
        "add_heads",
        functools.partial(add_heads_kernel, n_ctx, row),
        [WHOLE] * (1 + len(recv)),
        [keep, *recv],
        after,
        out_specs=[WHOLE] * n_ctx,
        out_shape=[jax.ShapeDtypeStruct((rows // n_ctx, width), BF16)] * n_ctx,
    )


def far_first(n):
    return sorted(range(1, n), key=lambda k: -min(k, n - k))


def send_sums(sums):
    n_ctx = len(sums)
    return [sums[0]] + [shift(sums[t], "ctx", n_ctx, -t) for t in far_first(n_ctx)]


def send_rows(x, n_ctx):
    got = {t: shift(x, "ctx", n_ctx, t) for t in far_first(n_ctx)}
    return [x] + [got[t] for t in range(1, n_ctx)]


def join_kernel(*refs):
    pieces, out_ref = refs[:-1], refs[-1]
    rows = pieces[0].shape[0]
    for t, ref in enumerate(pieces):
        out_ref[t * rows : (t + 1) * rows, :] = ref[...]


def join(pieces, after):
    rows, width = pieces[0].shape
    return run(
        "join",
        join_kernel,
        [WHOLE] * len(pieces),
        pieces,
        after,
        out_specs=WHOLE,
        out_shape=jax.ShapeDtypeStruct((rows * len(pieces), width), BF16),
    )


def state_kernel(n_pieces, *refs):
    pieces, (res_ref, gain_ref, state_ref, msg_ref) = refs[:n_pieces], refs[n_pieces:]
    width = res_ref.shape[1]
    total = res_ref[...].astype(F32)
    for ref in pieces:
        total = total + ref[...].astype(F32)
    state = total.astype(BF16)
    state_ref[...] = state
    wide = state.astype(F32)
    msg_ref[:, :width] = (wide * gain_ref[...]).astype(BF16)
    hi, mid, low = split3(jnp.sum(wide * wide, axis=1, keepdims=True))
    lane = lax.broadcasted_iota(jnp.int32, (hi.shape[0], HD), 1)
    stats = jnp.where(
        lane == 0, hi, jnp.where(lane == 1, mid, jnp.where(lane == 2, low, 0.0))
    )
    msg_ref[:, width:] = stats.astype(BF16)


def make_state(pieces, residual, gain, after):
    rows, width = residual.shape
    return run(
        "state",
        functools.partial(state_kernel, len(pieces)),
        [WHOLE] * (len(pieces) + 2),
        [*pieces, residual, gain],
        after,
        out_specs=[WHOLE] * 2,
        out_shape=[
            jax.ShapeDtypeStruct((rows, width), BF16),
            jax.ShapeDtypeStruct((rows, width + HD), BF16),
        ],
        cost_estimate=cost(8),
    )


def finish_kernel(above, *refs):
    terms, out_ref = refs[above:-1], refs[-1]
    total = terms[0][...].astype(F32)
    for ref in terms[1:]:
        total = total + ref[...].astype(F32)
    row = 0
    for ref in refs[:above]:
        out_ref[row : row + ref.shape[0], :] = ref[...]
        row += ref.shape[0]
    out_ref[row:, :] = total.astype(out_ref.dtype)


def finish(pieces, above=()):
    total = pieces[-1]
    for i in reversed(range(len(pieces) - 1)):
        on_top = list(above) if i == 0 else []
        rows, width = total.shape
        shape = (sum(x.shape[0] for x in on_top) + rows, width)
        total = run(
            "finish",
            functools.partial(finish_kernel, len(on_top)),
            [WHOLE] * (len(on_top) + 2),
            [*on_top, total, pieces[i]],
            out_specs=WHOLE,
            out_shape=jax.ShapeDtypeStruct(shape, F32 if i else BF16),
        )
    return total


def gate_up_kernel(chunks, n_parts, where_ref, *refs):
    parts, (g_hbm, u_hbm, out_ref, x, acc, g_buf, u_buf, g_sem, u_sem) = (
        refs[:n_parts],
        refs[n_parts:],
    )
    tile, units = g_buf.shape[1:]
    at = pl.multiple_of(where_ref[0] * units, 128)

    def chunk_copy(i, which):
        hbm, buf, sem = ((g_hbm, g_buf, g_sem), (u_hbm, u_buf, u_sem))[which]
        from_at = pl.multiple_of(i * tile, tile)
        return pltpu.make_async_copy(
            hbm.at[pl.ds(from_at, tile), pl.ds(at, units)], buf.at[i], sem.at[i]
        )

    for i in range(chunks):
        chunk_copy(i, 0).start()
        chunk_copy(i, 1).start()
    row = 0
    for ref in parts:
        x[row : row + ref.shape[0]] = ref[:, : x.shape[1]]
        row += ref.shape[0]
    acc[...] = jnp.zeros_like(acc)
    turns = 2

    @pl.loop(0, turns)
    def _(turn):
        gate = up = None
        for j in range(chunks // turns):
            i = turn * (chunks // turns) + j
            lhs = x[:, pl.ds(pl.multiple_of(i * tile, tile), tile)]
            chunk_copy(i, 0).wait()
            term = dot(lhs, g_buf[i])
            gate = term if gate is None else gate + term
            chunk_copy(i, 1).wait()
            term = dot(lhs, u_buf[i])
            up = term if up is None else up + term
        acc[:, :units] += gate
        acc[:, units:] += up

    out_ref[:, : 2 * units] = acc[...].astype(out_ref.dtype)
    row = 0
    for ref in parts:
        out_ref[row : row + ref.shape[0], 2 * units :] = ref[:, x.shape[1] :].astype(
            out_ref.dtype
        )
        row += ref.shape[0]


def gate_up(block, parts, gate_matrix, w_up, units, dtype, after=()):
    rows, depth = sum(p.shape[0] for p in parts), gate_matrix.shape[0]
    chunks = 8
    tile = depth // chunks
    return run(
        "gate_up",
        functools.partial(gate_up_kernel, chunks, len(parts)),
        [SCALARS] + [WHOLE] * len(parts) + [IN_PLACE] * 2,
        [block.reshape(1), *parts, gate_matrix, w_up],
        after,
        out_specs=WHOLE,
        out_shape=jax.ShapeDtypeStruct((rows, 2 * units + HD), dtype),
        scratch_shapes=[pltpu.VMEM((rows, depth), BF16), pltpu.VMEM((rows, 2 * units), F32)]
        + [pltpu.VMEM((chunks, tile, units), BF16)] * 2
        + [pltpu.SemaphoreType.DMA((chunks,))] * 2,
        cost_estimate=cost(6 if dtype == BF16 else 1),
    )


def act_kernel(own_ref, *refs):
    recv, out_ref = refs[:-1], refs[-1]
    total = own_ref[...]
    for ref in recv:
        total = total + ref[...].astype(F32)
    units = out_ref.shape[1]
    square = jnp.sum(total[:, 2 * units :], axis=1, keepdims=True)
    factor = lax.rsqrt(square / D + EPSILON)
    gate = factor * total[:, :units]
    up = factor * total[:, units : 2 * units]
    out_ref[...] = (gate / (1.0 + jnp.exp(-gate)) * up).astype(BF16)


def activate(own, recv, units, after):
    return run(
        "activate",
        act_kernel,
        [WHOLE] * (1 + len(recv)),
        [own, *recv],
        after,
        out_specs=WHOLE,
        out_shape=jax.ShapeDtypeStruct((own.shape[0], units), BF16),
    )


def down_kernel(n_parts, chunks, has_acc, last, n_head, where_ref, *refs):
    xs, refs = refs[:n_parts], refs[n_parts:]
    if has_acc:
        acc_ref, w_hbm, *outs, w_buf, sems = refs
    else:
        w_hbm, *outs, w_buf, sems = refs
    units, tile = w_buf.shape[2:]
    copies = []
    for i in range(chunks):
        for p in range(n_parts):
            at = pl.multiple_of(where_ref[p] * units, 16)
            copies.append(
                pltpu.make_async_copy(
                    w_hbm.at[pl.ds(at, units), pl.ds(i * tile, tile)],
                    w_buf.at[i, p],
                    sems.at[i, p],
                )
            )
    for copy in copies:
        copy.start()
    for i in range(chunks):
        total = acc_ref[:, i * tile : (i + 1) * tile] if has_acc else None
        for p in range(n_parts):
            copies[i * n_parts + p].wait()
            term = dot(xs[p][...], w_buf[i, p])
            total = term if total is None else total + term
        if last:
            per = total.shape[0] // n_head
            for b in range(n_head):
                outs[b][:, i * tile : (i + 1) * tile] = total[
                    b * per : (b + 1) * per
                ].astype(BF16)
        else:
            outs[0][:, i * tile : (i + 1) * tile] = total


def down(blocks, xs, w_down, acc, last, n_head, after):
    rows, units = xs[0].shape
    width = w_down.shape[1]
    chunks = 8
    tile = width // chunks
    n = len(xs)
    args = list(xs) + ([] if acc is None else [acc])
    if last:
        out_shape = [jax.ShapeDtypeStruct((rows // n_head, width), BF16)] * n_head
    else:
        out_shape = [jax.ShapeDtypeStruct((rows, width), F32)]
    out = run(
        "down",
        functools.partial(down_kernel, n, chunks, acc is not None, last, n_head),
        [SCALARS] + [WHOLE] * len(args) + [IN_PLACE],
        [jnp.stack(blocks), *args, w_down],
        after,
        out_specs=[WHOLE] * len(out_shape),
        out_shape=out_shape,
        scratch_shapes=[
            pltpu.VMEM((chunks, n, units, tile), BF16),
            pltpu.SemaphoreType.DMA((chunks, n)),
        ],
        cost_estimate=cost(4 * n),
    )
    return out if last else out[0]


def on_device(
    n_ctx,
    n_smp,
    n_head,
    queries,
    prefix_cache,
    suffix_cache,
    suffix_length,
    cache_sample,
    residual,
    w_out,
    norm_gain,
    gate_matrix,
    w_up,
    w_down,
):
    ctx, smp, head = (lax.axis_index(name) for name in ("ctx", "smp", "head"))
    samples = queries.shape[0]
    own_rows = residual.shape[0]
    queries = queries.reshape(samples, -1)
    prefix = prefix_cache.reshape(2, prefix_cache.shape[1], -1)
    rows, span = suffix_cache.shape[1:3]
    suffix = suffix_cache.reshape(2, rows, span, -1)
    kv_heads = prefix.shape[2] // HD
    group = QUERY_HEADS // KEY_VALUE_HEADS
    heads = kv_heads * group // n_ctx

    base = (ctx * n_smp + smp) * rows
    where = jnp.stack([ctx, smp, head, base])
    pieces = []
    for k in far_first(n_ctx) + [0]:
        piece = attention_piece(
            k, where, cache_sample, suffix_length, queries, prefix, suffix, heads, group
        )
        pieces.append(shift(piece, "ctx", n_ctx, k) if k else piece)

    parts = 2 if own_rows % 32 == 0 else 1
    step = own_rows // parts
    every = range(parts)
    others = range(1, n_smp)
    attn = merge(pieces, heads)
    gathered = [attn] + [shift(attn, "smp", n_smp, k) for k in others]
    by_head = project(where, gathered, w_out, n_ctx, n_head, own_rows, parts)
    all_sums = []
    for p in every:
        per = by_head[p].shape[0]
        sends = [x[p * per : (p + 1) * per] for x in by_head[parts:]]
        all_sums.append(add_heads(by_head[p], send_heads(sends, 1), 0, n_ctx))
    units = gate_matrix.shape[1] // n_smp
    states, rows, full = [None] * parts, [None] * parts, [None] * parts
    received, own, hidden, theirs, acc = ([None] * parts for _ in range(5))
    sums = [None] * parts
    done = []

    def state_step(p):
        nonlocal done
        states[p], message = make_state(
            send_sums(all_sums[p]), residual[p * step : (p + 1) * step], gain, done
        )
        rows[p] = send_rows(message, n_ctx)
        done = [states[p]]

    def others_step(p):
        nonlocal done
        joined = join(rows[p], done)
        full[p] = [shift(joined, "head", n_head, b) if b else joined for b in range(n_head)]
        received[p] = []
        for k in others:
            block = (smp + k) % n_smp
            send = gate_up(block, full[p], gate_matrix, w_up, units, BF16, done)
            done = [send]
            received[p].append(shift(send, "smp", n_smp, k))

    def own_step(p):
        nonlocal done
        own[p] = gate_up(smp, full[p], gate_matrix, w_up, units, F32, done)
        done = [own[p]]

    def hidden_step(p):
        nonlocal done
        hidden[p] = activate(own[p], received[p], units, done)
        theirs[p] = [shift(hidden[p], "smp", n_smp, k) for k in others]
        done = [hidden[p]]

    blocks = [(smp + n_smp - k) % n_smp for k in range(n_smp)]

    def down_step(p, first, count, acc):
        nonlocal done
        xs = [hidden[p], *theirs[p]][first : first + count]
        last = first + count == n_smp
        out = down(blocks[first : first + count], xs, w_down, acc, last, n_head, done)
        done = [out[0] if last else out]
        return out

    gain = norm_gain[None, :]
    state_step(0)
    for p in every:
        others_step(p)
        if p + 1 < parts:
            state_step(p + 1)
            own_step(p)
            hidden_step(p)
            acc[p] = down_step(p, 0, 1, None)
            continue
        own_step(p)
        by_head = [down_step(q, 1, n_smp - 1, acc[q]) for q in range(p)]
        hidden_step(p)
        for q, (keep, *sends) in enumerate(by_head):
            sums[q] = add_heads(keep, send_heads(sends, 1), 0, n_ctx, done)
        acc[p] = down_step(p, 0, 1, None)
        outs = [finish([states[q], *send_sums(sums[q])]) for q in range(p)]
        keep, *sends = down_step(p, 1, n_smp - 1, acc[p])
    sums[-1] = add_heads(keep, send_heads(sends, PIECES), 0, n_ctx, outs)
    return finish([states[-1], *send_sums(sums[-1])], outs)


def solution(mesh):
    in_specs = (
        P(("group", "smp"), "head", None),
        P(None, ("group", "ctx"), "head", None),
        P(None, ("group", "ctx", "smp"), None, "head", None),
        P(("group", "smp")),
        P("group"),
        P(("group", "ctx", "head"), "smp"),
        P("head", "ctx", "smp"),
        P("smp"),
        P("smp", ("ctx", "head")),
        P("smp", ("ctx", "head")),
        P(("ctx", "head"), "smp"),
    )
    out_specs = P(("group", "ctx", "head"), "smp")
    body = functools.partial(
        on_device, mesh.shape["ctx"], mesh.shape["smp"], mesh.shape["head"]
    )
    return jax.shard_map(
        body, mesh=mesh, in_specs=in_specs, out_specs=out_specs, check_vma=False
    )
```
